256 devices in a mesh: gx: 4 (over z_hi), gy: 16 (over y, z_lo, core), gz: 4 (over x).
Axes of the slice: x: 4, y: 4, z: 8 (z_hi: 4, z_lo: 2; z = z_hi * 2 + z_lo), core: 2. Of those that a mesh axis runs over, the one named last changes fastest.
Arguments:
- fraction: float32 [3, 4, 16, 4, 65536], P(None, 'gx', 'gy', 'gz'), may hold values from 0 to 1
- velocity: float32 [3, 4, 16, 4, 65536], P(None, 'gx', 'gy', 'gz'), may hold values from -1.2 to 1.2
- charge: float32 [4, 16, 4, 65536], P('gx', 'gy', 'gz'), may hold values from -1 to 1
- bead_type: int32 [4, 16, 4, 65536], P('gx', 'gy', 'gz'), may hold values from 0 to 17
- well_depth: float32 [18, 18], replicated, may hold values from 2 to 5.6
- tile_list: int32 [4, 16, 4, 1024, 2], P('gx', 'gy', 'gz'), may hold values from -1 to 866, as said below
- leaving: int32 [4, 16, 4, 6, 128], P('gx', 'gy', 'gz'), may hold values from -1 to 65535, as said below
Outputs:
- new_position: float32 [3, 4, 16, 4, 66304], P(None, 'gx', 'gy', 'gz')
- new_velocity: float32 [3, 4, 16, 4, 66304], P(None, 'gx', 'gy', 'gz')
The draws below stay inside these ranges and needn't reach their ends.
Inputs may be any that keep to these rules, and one draw needn't show every extreme that they name: `tile_list`: on each brick the live tiles come first and the rest are -1; a brick has between 512 and 1024 live tiles, and some brick has 1024. A live tile (i, j) has i <= j, and the two clusters' cells in the extended box differ by at most one along each axis, with the coordinatewise lower corner of the two cells a home cell. No tile repeats. The last gz brick lists no tile with a +z ghost. `leaving`: for each brick and face the live entries come first, the rest are -1; the live entries of a brick are distinct home slots over all six faces; a face has at most 128 live entries, and each brick has a face with exactly 128 unless the drawn face leads out of the slab; faces leading out of the slab (-z on the first gz brick, +z on the last) are all -1.
All inputs are finite; a program needn't handle non-finite values.
Results may differ from the reference program's by a relative error of at most 0.0003.
Values sent between devices are 32-bit elements; how exact they have to be, the bound alone decides.
No kernel may reach another device: no remote copies, remote signals or barrier semaphores. Data moves between devices by JAX's collectives and lax.ppermute only.
A program may use at most 128 MiB of HBM per device.

```python
import math
import jax
import jax.numpy as jnp
import numpy as np
from jax import lax

CELLS_ALONG_X = 16
CELLS_ALONG_Y = 2
CELLS_ALONG_Z = 16
NT = 18
TILES = 1024
MIG = 128
CELL_TOTAL = 512
HOME = 65536
FACE_X_GHOSTS = 32
FACE_Y_GHOSTS = 272
FACE_Z_GHOSTS = 51
GHOSTC = 355
ARRIVE = 768
BRICKS_X = 4
BRICKS_Y = 16
BRICKS_Z = 4


def box_cluster(cell_column_x, cell_column_y, cell_column_z):
    if cell_column_x < CELLS_ALONG_X and cell_column_y < CELLS_ALONG_Y and (cell_column_z < CELLS_ALONG_Z):
        return (cell_column_x * CELLS_ALONG_Y + cell_column_y) * CELLS_ALONG_Z + cell_column_z
    if cell_column_z == CELLS_ALONG_Z:
        return CELL_TOTAL + FACE_X_GHOSTS + FACE_Y_GHOSTS + cell_column_x * (CELLS_ALONG_Y + 1) + cell_column_y
    if cell_column_y == CELLS_ALONG_Y:
        return CELL_TOTAL + FACE_X_GHOSTS + cell_column_x * CELLS_ALONG_Z + cell_column_z
    return CELL_TOTAL + cell_column_y * CELLS_ALONG_Z + cell_column_z


def candidate_tiles():
    first_rows = []
    second_rows = []
    upward_rows = []
    for cell_column_x in range(CELLS_ALONG_X + 1):
        for cell_column_y in range(CELLS_ALONG_Y + 1):
            for cell_column_z in range(CELLS_ALONG_Z + 1):
                anchor = box_cluster(cell_column_x, cell_column_y, cell_column_z)
                for step_x in (-1, 0, 1):
                    for step_y in (-1, 0, 1):
                        for step_z in (-1, 0, 1):
                            other_x = cell_column_x + step_x
                            other_y = cell_column_y + step_y
                            other_z = cell_column_z + step_z
                            if not (0 <= other_x <= CELLS_ALONG_X and 0 <= other_y <= CELLS_ALONG_Y and (0 <= other_z <= CELLS_ALONG_Z)):
                                continue
                            if not (min(cell_column_x, other_x) < CELLS_ALONG_X and min(cell_column_y, other_y) < CELLS_ALONG_Y and (min(cell_column_z, other_z) < CELLS_ALONG_Z)):
                                continue
                            other = box_cluster(other_x, other_y, other_z)
                            if other >= anchor:
                                first_rows.append(anchor)
                                second_rows.append(other)
                                upward_rows.append(1 if cell_column_z == CELLS_ALONG_Z or other_z == CELLS_ALONG_Z else 0)
    return (np.array(first_rows, np.int32), np.array(second_rows, np.int32), np.array(upward_rows, np.int32))


def draw_tile_list(key, part):
    key = jax.random.fold_in(key, 11)
    first_np, second_np, upward_np = candidate_tiles()
    total = first_np.shape[0]
    devices_total = BRICKS_X * BRICKS_Y * BRICKS_Z
    rank_keys = jax.random.split(jax.random.fold_in(key, 1), devices_total)
    ranks = jax.vmap(lambda sub_key: jax.random.permutation(sub_key, total))(rank_keys).astype(jnp.int32)
    layer = jnp.arange(devices_total, dtype=jnp.int32) % BRICKS_Z
    barred = (layer == BRICKS_Z - 1)[:, None] & (jnp.asarray(upward_np) == 1)[None, :]
    score = ranks + total * barred.astype(jnp.int32)
    order = jnp.argsort(score, axis=1, stable=True)[:, :TILES]
    picked_first = jnp.asarray(first_np)[order]
    picked_second = jnp.asarray(second_np)[order]
    counts = jax.random.randint(jax.random.fold_in(key, 2), (devices_total,), TILES // 2, TILES + 1)
    fullest = jax.random.randint(jax.random.fold_in(key, 3), (), 0, devices_total)
    counts = jnp.where(jnp.arange(devices_total) == fullest, TILES, counts)
    alive = jnp.arange(TILES)[None, :] < counts[:, None]
    result = jnp.stack([jnp.where(alive, picked_first, -1), jnp.where(alive, picked_second, -1)], axis=-1)
    return result.astype(jnp.int32).reshape(BRICKS_X, BRICKS_Y, BRICKS_Z, TILES, 2)


def draw_leaving(key, part):
    key = jax.random.fold_in(key, 23)
    devices_total = BRICKS_X * BRICKS_Y * BRICKS_Z
    slot_keys = jax.random.split(jax.random.fold_in(key, 1), devices_total)
    slots = jax.vmap(lambda sub_key: jax.random.permutation(sub_key, HOME))(slot_keys)[:, :6 * MIG]
    slots = slots.astype(jnp.int32).reshape(devices_total, 6, MIG)
    counts = jax.random.randint(jax.random.fold_in(key, 2), (devices_total, 6), MIG // 4, MIG + 1)
    fullface = jax.random.randint(jax.random.fold_in(key, 3), (devices_total,), 0, 6)
    faces = jnp.arange(6)[None, :]
    counts = jnp.where(faces == fullface[:, None], MIG, counts)
    layer = (jnp.arange(devices_total) % BRICKS_Z)[:, None]
    counts = jnp.where((faces == 4) & (layer == 0), 0, counts)
    counts = jnp.where((faces == 5) & (layer == BRICKS_Z - 1), 0, counts)
    alive = jnp.arange(MIG)[None, None, :] < counts[:, :, None]
    result = jnp.where(alive, slots, -1)
    return result.astype(jnp.int32).reshape(BRICKS_X, BRICKS_Y, BRICKS_Z, 6, MIG)


def place_ends(entries, stream_key, least, largest):
    index_at = [jax.random.randint(jax.random.fold_in(stream_key, axis), (), 0, length) for axis, length in enumerate(entries.shape)]
    longest = entries.shape.index(max(entries.shape))
    beside = index_at[:longest] + [(index_at[longest] + 1) % entries.shape[longest]] + index_at[longest + 1:]
    return entries.at[tuple(index_at)].set(least).at[tuple(beside)].set(largest)


def steps_of(key, extent, cuts, least, largest):
    def one(dim, blocks):
        draws = jax.random.uniform(jax.random.fold_in(jax.random.fold_in(key, 6), dim), (blocks,), jnp.float32, least / len(cuts), largest / len(cuts))
        return jnp.repeat(jnp.exp(draws), extent[dim] // blocks).reshape((-1,) + (1,) * (len(extent) - dim - 1))

    gain = one(*cuts[0])
    for cut in cuts[1:]:
        gain = gain * one(*cut)
    return gain


def scatter_about(rng, dims, scale, limit, cuts=(), kind=jnp.bfloat16):
    entries = scale * jax.random.normal(rng, dims, jnp.float32)
    if cuts:
        entries = entries * steps_of(rng, dims, cuts, -0.22, 0.18)
    return jnp.clip(entries, -limit, limit).astype(kind)


def setup_inputs(seed: int = 0) -> dict:
    streams_of = jax.random.split(jax.random.key(seed), 8)
    return {
        "fraction": jnp.clip(1.0 * jax.random.uniform(streams_of[0], (3, BRICKS_X, BRICKS_Y, BRICKS_Z, HOME), jnp.float32) ** steps_of(streams_of[0], (3, BRICKS_X, BRICKS_Y, BRICKS_Z, HOME), ((1, 4), (2, 16), (3, 4)), -0.2, 0.2), 0.0, 1.0),
        "velocity": scatter_about(streams_of[1], (3, BRICKS_X, BRICKS_Y, BRICKS_Z, HOME), 0.2, 1.2, ((1, 4), (2, 16), (3, 4)), jnp.float32),
        "charge": jnp.clip(jax.random.uniform(streams_of[2], (BRICKS_X, BRICKS_Y, BRICKS_Z, HOME), jnp.float32, -1.0, 1.0) * steps_of(streams_of[2], (BRICKS_X, BRICKS_Y, BRICKS_Z, HOME), ((0, 4), (1, 16), (2, 4)), -0.4, 0.0), -1.0, 1.0),
        "bead_type": place_ends(jax.random.randint(streams_of[3], (BRICKS_X, BRICKS_Y, BRICKS_Z, HOME), 0, NT), jax.random.fold_in(streams_of[3], 1), 0, NT - 1).astype(jnp.int32),
        "well_depth": jnp.clip(jnp.exp(jax.random.uniform(streams_of[4], (NT, NT), jnp.float32, math.log(2.0), math.log(5.6))), 2.0, 5.6),
        "tile_list": draw_tile_list(jax.random.fold_in(streams_of[7], 71), 0),
        "leaving": draw_leaving(jax.random.fold_in(streams_of[7], 71), 0),
    }


CELL_X = 4.0
CELL_Y = 2.0
CELL_Z = 2.0
CUTOFF2 = 1.21
SIGMA2 = 0.2209
FLOOR2 = 0.1764
EDGE_C = (SIGMA2 / CUTOFF2) ** 3
LJ_EDGE = 24.0 * EDGE_C * (2.0 * EDGE_C - 1.0) / CUTOFF2
COULOMB = 138.935458 / 2.5
INV_CUT3 = 1.0 / 1.331
STEP = 0.03
KICK = 0.03 / 144.0
batches = 8

def tile_forces(first_data, first_kind, second_data, second_kind, same_tile, table):
    labels = jnp.arange(table.shape[0], dtype=jnp.int32)
    delta = first_data[:, :3, :, None] - second_data[:, :3, None, :]
    dist2 = lax.optimization_barrier(jnp.sum(delta * delta, axis=1))
    soft2 = jnp.maximum(dist2, FLOOR2)
    inverse2 = 1.0 / soft2
    sixth = (SIGMA2 * inverse2) ** 3
    first_hot = (first_kind[:, :, None] == labels).astype(jnp.float32)
    second_hot = (second_kind[:, :, None] == labels).astype(jnp.float32)
    depth = jnp.einsum('nak,kl,nbl->nab', first_hot, table, second_hot, precision=lax.Precision.HIGHEST)
    lennard = depth * (24.0 * inverse2 * sixth * (2.0 * sixth - 1.0) - LJ_EDGE)
    product = first_data[:, 3, :, None] * second_data[:, 3, None, :]
    coulomb = COULOMB * product * (inverse2 * lax.rsqrt(soft2) - INV_CUT3)
    width = first_data.shape[2]
    upper = jnp.arange(width)[:, None] < jnp.arange(width)[None, :]
    keep = (dist2 < CUTOFF2) & (jnp.logical_not(same_tile)[:, None, None] | upper[None])
    scalar = jnp.where(keep, lennard + coulomb, 0.0)
    weighted = scalar[:, None] * delta
    return (lax.optimization_barrier(jnp.sum(weighted, axis=3)), -lax.optimization_barrier(jnp.sum(weighted, axis=2)))

def run_tiles(pair_forces, cluster_data, cluster_kind, tile_rows, count, table, every):
    batch = tile_rows.shape[0] // batches

    def advance(turn, totals):
        rows = lax.dynamic_slice_in_dim(tile_rows, turn * batch, batch, 0)
        first = rows[:, 0]
        second = rows[:, 1]
        weight = (first >= 0).astype(totals.dtype)[:, None, None]
        first_safe = jnp.maximum(first, 0)
        second_safe = jnp.maximum(second, 0)
        on_first, on_second = tile_forces(cluster_data[first_safe], cluster_kind[first_safe], cluster_data[second_safe], cluster_kind[second_safe], first == second, table)
        return totals.at[first_safe].add(on_first * weight).at[second_safe].add(on_second * weight)
    if every:
        stop = batches
    else:
        stop = (count + batch - 1) // batch
    return lax.fori_loop(0, stop, advance, pair_forces)

def reference(fraction, velocity, charge, bead_type, well_depth, tile_list, leaving):
    table = 0.5 * (well_depth + well_depth.T)
    dtype = fraction.dtype
    devices_total = BRICKS_X * BRICKS_Y * BRICKS_Z
    cell_lattice = (BRICKS_X, BRICKS_Y, BRICKS_Z)
    shape_cells = cell_lattice + (CELLS_ALONG_X, CELLS_ALONG_Y, CELLS_ALONG_Z, 128)
    frac = fraction.reshape((3,) + shape_cells)
    index_x = jnp.arange(CELLS_ALONG_X).astype(dtype).reshape(CELLS_ALONG_X, 1, 1, 1)
    index_y = jnp.arange(CELLS_ALONG_Y).astype(dtype).reshape(CELLS_ALONG_Y, 1, 1)
    index_z = jnp.arange(CELLS_ALONG_Z).astype(dtype).reshape(CELLS_ALONG_Z, 1)
    coord_x = (index_x + frac[0]) * CELL_X
    coord_y = (index_y + frac[1]) * CELL_Y
    coord_z = (index_z + frac[2]) * CELL_Z
    kind_value = bead_type.reshape(shape_cells).astype(dtype)
    cluster_payload = jnp.stack([coord_x, coord_y, coord_z, charge.reshape(shape_cells), kind_value], axis=-2)
    span_x = CELLS_ALONG_X * CELL_X
    span_y = CELLS_ALONG_Y * CELL_Y
    span_z = CELLS_ALONG_Z * CELL_Z
    received_x = jnp.roll(cluster_payload, -1, axis=0)[:, :, :, 0]
    received_x = received_x.at[..., 0, :].add(span_x)
    plane_xy = jnp.concatenate([cluster_payload, received_x[:, :, :, None]], axis=3)
    received_y = jnp.roll(plane_xy[:, :, :, :, 0], -1, axis=1)
    received_y = received_y.at[..., 1, :].add(span_y)
    ghost_box = jnp.concatenate([plane_xy, received_y[:, :, :, :, None]], axis=4)
    inside = (jnp.arange(BRICKS_Z) < BRICKS_Z - 1).reshape(1, 1, BRICKS_Z, 1, 1, 1, 1)
    received_z = jnp.roll(ghost_box[:, :, :, :, :, 0], -1, axis=2)
    received_z = jnp.where(inside, received_z, 0.0).at[..., 2, :].add(span_z)
    widened_grid = jnp.concatenate([cluster_payload.reshape(cell_lattice + (CELL_TOTAL, 5, 128)), received_x.reshape(cell_lattice + (FACE_X_GHOSTS, 5, 128)), received_y.reshape(cell_lattice + (FACE_Y_GHOSTS, 5, 128)), received_z.reshape(cell_lattice + (FACE_Z_GHOSTS, 5, 128))], axis=3)
    widened_grid = widened_grid.reshape(devices_total, CELL_TOTAL + GHOSTC, 5, 128)
    extended_kind = widened_grid[:, :, 4].astype(jnp.int32)
    lists = tile_list.reshape(devices_total, TILES, 2)
    empty = jnp.zeros((CELL_TOTAL + GHOSTC, 3, 128), dtype)

    def device_force(bundle):
        return run_tiles(empty, bundle[0], bundle[1], bundle[2], 0, table, True)
    pair_forces = lax.map(device_force, (widened_grid, extended_kind, lists))
    pair_forces = pair_forces.reshape(cell_lattice + (CELL_TOTAL + GHOSTC, 3, 128))
    home_force = pair_forces[:, :, :, :CELL_TOTAL].reshape(cell_lattice + (CELLS_ALONG_X, CELLS_ALONG_Y, CELLS_ALONG_Z, 3, 128))
    ghost_force_x = pair_forces[:, :, :, CELL_TOTAL:CELL_TOTAL + FACE_X_GHOSTS].reshape(cell_lattice + (1, CELLS_ALONG_Y, CELLS_ALONG_Z, 3, 128))
    ghost_force_y = pair_forces[:, :, :, CELL_TOTAL + FACE_X_GHOSTS:CELL_TOTAL + FACE_X_GHOSTS + FACE_Y_GHOSTS].reshape(cell_lattice + (CELLS_ALONG_X + 1, 1, CELLS_ALONG_Z, 3, 128))
    ghost_force_z = pair_forces[:, :, :, CELL_TOTAL + FACE_X_GHOSTS + FACE_Y_GHOSTS:].reshape(cell_lattice + (CELLS_ALONG_X + 1, CELLS_ALONG_Y + 1, 3, 128))
    force_box = jnp.concatenate([jnp.concatenate([home_force, ghost_force_x], axis=3), ghost_force_y], axis=4)
    below = (jnp.arange(BRICKS_Z) > 0).reshape(1, 1, BRICKS_Z, 1, 1, 1, 1)
    back_z = jnp.where(below, jnp.roll(ghost_force_z, 1, axis=2), 0.0)
    force_box = force_box.at[:, :, :, :, :, 0].add(back_z)
    back_y = jnp.roll(force_box[:, :, :, :, CELLS_ALONG_Y], 1, axis=1)
    force_box = force_box.at[:, :, :, :, 0].add(back_y)
    back_x = jnp.roll(force_box[:, :, :, CELLS_ALONG_X, :CELLS_ALONG_Y], 1, axis=0)
    own = force_box[:, :, :, :CELLS_ALONG_X, :CELLS_ALONG_Y].at[:, :, :, 0].add(back_x)
    total = jnp.moveaxis(own, 6, 0).reshape((3,) + cell_lattice + (HOME,))
    place = jnp.moveaxis(cluster_payload[..., :3, :], 6, 0).reshape((3,) + cell_lattice + (HOME,))
    half_velocity = velocity + KICK * total
    moved = place + STEP * half_velocity
    bundle_all = jnp.concatenate([moved, half_velocity], axis=0)
    alive = leaving >= 0
    safe = jnp.maximum(leaving, 0)
    picked = jnp.take_along_axis(bundle_all, safe.reshape((1,) + cell_lattice + (6 * MIG,)), axis=-1)
    picked = picked.reshape((6,) + cell_lattice + (6, MIG))
    frame = jnp.array([[span_x, -span_x, 0.0, 0.0, 0.0, 0.0], [0.0, 0.0, span_y, -span_y, 0.0, 0.0], [0.0, 0.0, 0.0, 0.0, span_z, -span_z], [0.0] * 6, [0.0] * 6, [0.0] * 6], dtype)
    sent = (picked + frame.reshape(6, 1, 1, 1, 6, 1)) * alive[None].astype(dtype)
    arrivals = jnp.stack([jnp.roll(sent[:, :, :, :, 0], -1, axis=1), jnp.roll(sent[:, :, :, :, 1], 1, axis=1), jnp.roll(sent[:, :, :, :, 2], -1, axis=2), jnp.roll(sent[:, :, :, :, 3], 1, axis=2), jnp.roll(sent[:, :, :, :, 4], -1, axis=3), jnp.roll(sent[:, :, :, :, 5], 1, axis=3)], axis=4).reshape((6,) + cell_lattice + (ARRIVE,))
    device_rows = jnp.arange(devices_total)[:, None]
    keep = jnp.ones((devices_total, HOME), dtype).at[device_rows, safe.reshape(devices_total, 6 * MIG)].min(jnp.logical_not(alive).reshape(devices_total, 6 * MIG).astype(dtype))
    keep = keep.reshape((1,) + cell_lattice + (HOME,))
    new_position = jnp.concatenate([moved * keep, arrivals[:3]], axis=-1)
    new_velocity = jnp.concatenate([half_velocity * keep, arrivals[3:]], axis=-1)
    return (new_position, new_velocity)
```

```python
import math
import jax
import jax.numpy as jnp
from jax import lax
from jax.experimental import pallas as pl
from jax.experimental.pallas import tpu as pltpu
from jax.sharding import PartitionSpec as P

CELLS = (16, 2, 16)
MIG = 128
HOME = 65536
ARRIVE = 768
STEP = 0.03
KICK = 0.03 / 144.0
BOX = (64.0, 4.0, 32.0)
C = 872
TILES = 1024
SPAN = (4.0, 2.0, 2.0)
CUTOFF2 = 1.21
NEAR2 = 1.2105
SIGMA2 = 0.2209
FLOOR2 = 0.1764
EDGE_C = (SIGMA2 / CUTOFF2) ** 3
LJ_EDGE = 24.0 * EDGE_C * (2.0 * EDGE_C - 1.0) / CUTOFF2
LJ_A = 48.0 * SIGMA2**6
LJ_B = 24.0 * SIGMA2**3
COULOMB = 138.935458 / 2.5
INV_CUT3 = 1.0 / 1.331
UNROLL = 6
ROWS = 16
f32 = jnp.float32
bf16 = jnp.bfloat16


def split3(x):
    hi = x.astype(bf16)
    rest = x - hi.astype(f32)
    mid = rest.astype(bf16)
    low = (rest - mid.astype(f32)).astype(bf16)
    return hi, mid, low


def dot_nt(a, b):
    return lax.dot_general(a, b, (((1,), (1,)), ((), ())), preferred_element_type=f32)


def force_kernel(code, live, home, gx, gy, gz, table, out, fields, near, dist, rank, cnt, acc_a, acc_b, counts, spread, picked, compact, sem):
    zero = jnp.zeros((8, 128), f32)

    def load(src, first, k):
        row = pl.multiple_of(8 * k, 8)
        to = pl.multiple_of(first + 8 * k, 8)
        for m in range(8):
            fields[pl.ds(pl.multiple_of(8 * to + 8 * m, 8), 8), :] = zero
        for m in range(24):
            acc_a[pl.ds(pl.multiple_of(24 * to + 8 * m, 8), 8), :] = zero
            acc_b[pl.ds(pl.multiple_of(24 * to + 8 * m, 8), 8), :] = zero
        for f in range(5):
            r = src[f, pl.ds(row, 8), :]
            fields[pl.ds(8 * to + f, 8, stride=8), :] = r
            if f < 3:
                s = SPAN[f] - r
                near[pl.ds(pl.multiple_of(3 * f * C + to, 8), 8), :] = r * r
                near[pl.ds(pl.multiple_of((3 * f + 1) * C + to, 8), 8), :] = zero
                near[pl.ds(pl.multiple_of((3 * f + 2) * C + to, 8), 8), :] = s * s
        return 0
    for src, first, count in ((home, 0, 512), (gx, 512, 32), (gy, 544, 272), (gz, 816, 56)):
        lax.fori_loop(0, count // 8, lambda k, _, src=src, first=first: load(src, first, k), 0)

    n_live = live[0]

    def stage(k, _):
        for m in range(8):
            w = code[8 * k + m]
            i = w & 1023
            ax = (w >> 20) & 3
            ay = (w >> 22) & 3
            az = (w >> 24) & 3
            s = (near[pl.ds(ax * C + i, 1), :] + near[pl.ds((3 + ay) * C + i, 1), :]
                 + near[pl.ds((6 + az) * C + i, 1), :])
            dist[pl.ds(8 * k + m, 1), :] = s
        return 0
    lax.fori_loop(0, (n_live + 7) // 8, stage, 0)

    below = (lax.broadcasted_iota(jnp.int32, (128, 128), 0)
             < lax.broadcasted_iota(jnp.int32, (128, 128), 1)).astype(f32).astype(bf16)
    row_id = lax.broadcasted_iota(jnp.int32, (128, 128), 0)
    ones = jnp.ones((16, 128), bf16)
    for g in range(TILES // 128):
        keep = (dist[128 * g:128 * g + 128, :] < NEAR2) & (row_id + 128 * g < n_live)
        hot = jnp.where(keep, 1.0, 0.0).astype(bf16)
        before = jnp.dot(hot, below, preferred_element_type=f32)
        rank[128 * g:128 * g + 128, :] = jnp.where(keep, before, -1.0)
        cnt[g:g + 1, :] = dot_nt(ones, hot)[0:1].astype(jnp.int32)
    rank[TILES:TILES + 8, :] = jnp.full((8, 128), -1.0, f32)
    cnt[TILES // 128:, :] = jnp.zeros((8, 128), jnp.int32)
    copy = pltpu.make_async_copy(cnt, counts, sem)
    copy.start()
    copy.wait()

    sub = lax.broadcasted_iota(jnp.int32, (ROWS, 128), 0).astype(f32)
    kinds = lax.broadcasted_iota(jnp.int32, (24, 128), 0).astype(f32)
    U = UNROLL

    wr = lax.broadcasted_iota(jnp.int32, (24, 128), 0)
    for f in range(4):
        spread[0:24, 128 * f:128 * f + 128] = jnp.where((wr & 7) == f, 1.0, 0.0)
        spread[24:96, 128 * f:128 * f + 128] = jnp.zeros((72, 128), f32)
    spread[0:24, 512:640] = jnp.zeros((24, 128), f32)
    for m, part in enumerate(split3(table[0:24, :])):
        spread[24 + 24 * m:48 + 24 * m, 512:640] = part.astype(f32)
    weights = spread[...].astype(bf16)

    def decode(t, off):
        info = []
        for u in range(U):
            tt = jnp.minimum(t, TILES)
            n = counts[tt >> 7, tt & 127]
            info.append(tt | off << 11)
            last = off + ROWS >= n
            t = jnp.where(last, t + 1, t)
            off = jnp.where(last, 0, off + ROWS)
        return tuple(info), t, off

    def chosen(tt, o):
        return rank[pl.ds(tt, ROWS, stride=0), :] == sub + o.astype(f32)

    def select(info):
        for u, word in enumerate(info):
            tt, o = word & 2047, word >> 11
            i = code[tt] & 1023
            hot = jnp.where(chosen(tt, o), 1.0, 0.0).astype(bf16)
            d = fields[pl.ds(pl.multiple_of(8 * i, 8), 8), :]
            hi = d.astype(bf16).astype(f32)
            mid = (d - hi).astype(bf16).astype(f32)
            kind = jnp.where(fields[pl.ds(8 * i + 4, 24, stride=0), :] == kinds, 1.0, 0.0)
            rows = jnp.concatenate([hi, mid, d - hi - mid, kind, kind, kind], axis=0)
            compact[ROWS * u:ROWS * u + ROWS, :] = dot_nt(hot, rows.astype(bf16)).astype(bf16)

    def widen():
        picked[...] = jnp.dot(compact[...], weights, preferred_element_type=f32)

    def interact(info):
        sums = []
        for u, word in enumerate(info):
            tt, o = word & 2047, word >> 11
            w = code[tt]
            i = w & 1023
            j = (w >> 10) & 1023
            at = slice(ROWS * u, ROWS * u + ROWS)
            ds = []
            for ax in range(3):
                step = (((w >> (20 + 2 * ax)) & 3) - 1).astype(f32) * SPAN[ax]
                pb = fields[pl.ds(8 * j + ax, 8, stride=0), :] + step
                ds.append(picked[at, 128 * ax:128 * ax + 128] - jnp.concatenate([pb, pb], axis=0))
            qb = fields[pl.ds(8 * j + 3, ROWS, stride=0), :]
            kb = fields[pl.ds(8 * j + 4, 8, stride=0), :].astype(jnp.int32)
            kb = jnp.concatenate([kb, kb], axis=0)
            e = jnp.take_along_axis(picked[at, 512:640], kb, axis=1)
            dx, dy, dz = ds
            r2 = dx * dx + dy * dy + dz * dz
            s2 = jnp.maximum(r2, FLOOR2)
            y = lax.rsqrt(s2)
            v = y * y
            v3 = v * v * v
            lj = (v3 - LJ_B / LJ_A) * (v3 * v) - LJ_EDGE / LJ_A
            g = e * lj + (picked[at, 384:512] * qb) * (v * y - INV_CUT3)
            half = jnp.where(i == j, 0.5, 1.0).astype(f32)
            g = jnp.where(r2 < CUTOFF2, g, 0.0) * half
            sel = chosen(tt, o)
            for f in range(3):
                ws = g * ds[f]
                row = jnp.where(sel, jnp.sum(ws, axis=1, keepdims=True), 0.0)
                sums.append((i, j, f, row[0:8] + row[8:16], ws[0:8] + ws[8:16]))
        for i, j, f, sa, sb in sums:
            at = pl.ds(pl.multiple_of(f * (8 * C) + i * 8, 8), 8)
            acc_a[at, :] = acc_a[at, :] + sa
            at = pl.ds(pl.multiple_of(f * (8 * C) + j * 8, 8), 8)
            acc_b[at, :] = acc_b[at, :] + sb

    def work(state):
        now, later, last, t, off = state
        new, t, off = decode(t, off)
        interact(now)
        widen()
        select(last)
        return later, last, new, t, off

    now, t0, off0 = decode(jnp.int32(0), jnp.int32(0))
    select(now)
    later, t0, off0 = decode(t0, off0)
    widen()
    select(later)
    last, t0, off0 = decode(t0, off0)
    lax.while_loop(lambda s: (s[0][0] & 2047) < n_live, work, (now, later, last, t0, off0))

    for f in range(3):
        def fold(k, _, f=f):
            base = f * (8 * C) + 64 * k
            a = acc_a[pl.ds(base, 8, stride=8), :]
            b = acc_b[pl.ds(base, 8, stride=8), :]
            for m in range(1, 8):
                a = a + acc_a[pl.ds(base + m, 8, stride=8), :]
                b = b + acc_b[pl.ds(base + m, 8, stride=8), :]
            out[f, pl.ds(pl.multiple_of(8 * k, 8), 8), :] = a - b
            return 0
        lax.fori_loop(0, C // 8, fold, 0)


def forces(code, live, home, gx, gy, gz, table):
    vm = pl.BlockSpec(memory_space=pltpu.VMEM)
    sm = pl.BlockSpec(memory_space=pltpu.SMEM)
    return pl.pallas_call(
        force_kernel,
        out_shape=jax.ShapeDtypeStruct((3, C, 128), f32),
        in_specs=[sm, sm, vm, vm, vm, vm, vm],
        out_specs=vm,
        scratch_shapes=[
            pltpu.VMEM((8 * C, 128), f32),
            pltpu.VMEM((9 * C, 128), f32),
            pltpu.VMEM((TILES, 128), f32),
            pltpu.VMEM((TILES + 32, 128), f32),
            pltpu.VMEM((16, 128), jnp.int32),
            pltpu.VMEM((24 * C, 128), f32),
            pltpu.VMEM((24 * C, 128), f32),
            pltpu.SMEM((16, 128), jnp.int32),
            pltpu.VMEM((96, 640), f32),
            pltpu.VMEM((ROWS * UNROLL, 640), f32),
            pltpu.VMEM((ROWS * UNROLL, 96), bf16),
            pltpu.SemaphoreType.DMA,
        ],
        compiler_params=pltpu.CompilerParams(vmem_limit_bytes=56 * 2**20),
        name="pair_forces",
    )(code, live, home, gx, gy, gz, table)


def advance_kernel(leaving, force, bx, by, bxy, bz, bxz, byz, bxyz, fraction, velocity, pos, vel, sent, total, beads):
    for f in range(3):
        total[f] = force[f, 0:512, :]
        total[f, 0:32, :] = total[f, 0:32, :] + bx[f]
        for k in range(16):
            total[f, 32 * k:32 * k + 16, :] = total[f, 32 * k:32 * k + 16, :] + by[f, 16 * k:16 * k + 16, :]
        total[f, 0:16, :] = total[f, 0:16, :] + bxy[f]
        for k in range(32):
            total[f, 16 * k:16 * k + 1, :] = total[f, 16 * k:16 * k + 1, :] + bz[f, k:k + 1, :]
        for k in range(16):
            total[f, 32 * k:32 * k + 1, :] = total[f, 32 * k:32 * k + 1, :] + byz[f, k:k + 1, :]
        for k in range(2):
            total[f, 16 * k:16 * k + 1, :] = total[f, 16 * k:16 * k + 1, :] + bxz[f, k:k + 1, :]
        total[f, 0:1, :] = total[f, 0:1, :] + bxyz[f]

    sub = lax.broadcasted_iota(jnp.int32, (8, 128), 0)
    lane = lax.broadcasted_iota(jnp.int32, (8, 128), 1)

    def move(k, _):
        rows = pl.ds(pl.multiple_of(8 * k, 8), 8)
        cluster = 8 * k + sub
        cells = (cluster >> 5, (cluster >> 4) & 1, cluster & 15)
        for f in range(3):
            half = velocity[f, rows, :] + KICK * total[f, rows, :]
            place = (cells[f].astype(f32) + fraction[f, rows, :]) * SPAN[f] + STEP * half
            beads[pl.ds(64 * k + f, 8, stride=8), :] = place
            beads[pl.ds(64 * k + 3 + f, 8, stride=8), :] = half
        return 0
    lax.fori_loop(0, 64, move, 0, unroll=2)

    for face in range(6):
        def pick(k, taken, face=face):
            for u in range(8):
                m = 8 * k + u
                slot = leaving[face * MIG + m]
                at = jnp.maximum(slot, 0)
                row = beads[pl.ds(pl.multiple_of((at >> 7) * 8, 8), 8), :]
                row = pltpu.roll(row, (m - at) & 127, 1)
                taken = jnp.where(lane == jnp.where(slot >= 0, m, -1), row, taken)
            return taken
        sent[face] = lax.fori_loop(0, MIG // 8, pick, jnp.zeros((8, 128), f32))

    def drop(k, _):
        for u in range(8):
            slot = leaving[8 * k + u]
            at = jnp.maximum(slot, 0)
            rows = pl.ds(pl.multiple_of((at >> 7) * 8, 8), 8)
            beads[rows, :] = jnp.where(lane == jnp.where(slot >= 0, at & 127, -1), 0.0, beads[rows, :])
        return 0
    lax.fori_loop(0, 6 * MIG // 8, drop, 0)

    def store(k, _):
        rows = pl.ds(pl.multiple_of(8 * k, 8), 8)
        for f in range(3):
            pos[f, rows, :] = beads[pl.ds(64 * k + f, 8, stride=8), :]
            vel[f, rows, :] = beads[pl.ds(64 * k + 3 + f, 8, stride=8), :]
        return 0
    lax.fori_loop(0, 64, store, 0, unroll=2)


def advance(leaving, *arrays):
    vm = pl.BlockSpec(memory_space=pltpu.VMEM)
    sm = pl.BlockSpec(memory_space=pltpu.SMEM)
    return pl.pallas_call(
        advance_kernel,
        out_shape=[
            jax.ShapeDtypeStruct((3, 512, 128), f32),
            jax.ShapeDtypeStruct((3, 512, 128), f32),
            jax.ShapeDtypeStruct((6, 8, 128), f32),
        ],
        in_specs=[sm] + [vm] * len(arrays),
        out_specs=[vm, vm, vm],
        scratch_shapes=[pltpu.VMEM((3, 512, 128), f32), pltpu.VMEM((4096, 128), f32)],
        compiler_params=pltpu.CompilerParams(vmem_limit_bytes=40 * 2**20),
        name="advance",
    )(leaving, *arrays)


def across(block, step):
    names = tuple(n for n, s in zip(("gx", "gy", "gz"), step) if s)
    steps = [s for s in step if s]
    sizes = [lax.axis_size(n) for n in names]
    pairs = []
    for flat in range(math.prod(sizes)):
        rest, source = flat, []
        for size in reversed(sizes):
            source.insert(0, rest % size)
            rest //= size
        target = 0
        inside = True
        for name, size, at, s in zip(names, sizes, source, steps):
            to = at + s
            if name == "gz" and not 0 <= to < size:
                inside = False
            target = target * size + to % size
        if inside:
            pairs.append((flat, target))
    return lax.ppermute(block, names if len(names) > 1 else names[0], pairs)


def cell_of(index):
    home = index < 512
    on_x = index < 544
    on_y = index < 816
    y, z = index - 544, index - 816
    bx = jnp.where(home, index >> 5, jnp.where(on_x, 16, jnp.where(on_y, y >> 4, z // 3)))
    by = jnp.where(home, (index >> 4) & 1, jnp.where(on_x, ((index - 512) >> 4) & 1, jnp.where(on_y, 2, z % 3)))
    bz = jnp.where(on_y, index & 15, 16)
    return bx, by, bz


def body(fraction, velocity, charge, bead_type, well_depth, tile_list, leaving):
    frac = fraction.reshape(3, 512, 128)
    span = jnp.array(SPAN, f32).reshape(3, 1, 1)
    data = jnp.concatenate(
        [
            frac * span,
            math.sqrt(COULOMB) * charge.reshape(1, 512, 128),
            (bead_type.reshape(1, 512, 128) + 1).astype(f32),
        ],
        axis=0,
    )
    table = jnp.pad((0.5 * LJ_A) * (well_depth + well_depth.T), ((1, 109), (1, 109)))
    tiles = tile_list.reshape(TILES, 2)
    first, second = tiles[:, 0], tiles[:, 1]
    live = jnp.sum((first >= 0).astype(jnp.int32)).reshape(1)
    first, second = jnp.maximum(first, 0), jnp.maximum(second, 0)
    code = first | second << 10
    for n, (a, b) in enumerate(zip(cell_of(first), cell_of(second))):
        code = code | (b - a + 1) << (20 + 2 * n)
    code = jnp.pad(code, (0, 128))

    cells = data.reshape(5, 16, 2, 16, 128)
    gx = across(cells[:, 0], (-1, 0, 0))
    gy = across(cells[:, :, 0], (0, -1, 0))
    gxy = across(cells[:, 0, 0], (-1, -1, 0))
    gz = across(cells[:, :, :, 0], (0, 0, -1))
    gxz = across(cells[:, 0, :, 0], (-1, 0, -1))
    gyz = across(cells[:, :, 0, 0], (0, -1, -1))
    gxyz = across(cells[:, 0, 0, 0], (-1, -1, -1))
    side_y = jnp.concatenate([gy.reshape(5, 256, 128), gxy], axis=1)
    side_z = jnp.concatenate(
        [
            jnp.concatenate([gz, gyz[:, :, None]], axis=2).reshape(5, 48, 128),
            gxz,
            gxyz[:, None],
            jnp.zeros((5, 5, 128), f32),
        ],
        axis=1,
    )
    force = forces(code, live, data, gx.reshape(5, 32, 128), side_y, side_z, table)

    low_z = force[:, 816:864].reshape(3, 16, 3, 128)
    back_x = across(force[:, 512:544], (1, 0, 0))
    back_y = across(force[:, 544:800], (0, 1, 0))
    back_xy = across(force[:, 800:816], (1, 1, 0))
    back_z = across(low_z[:, :, :2].reshape(3, 32, 128), (0, 0, 1))
    back_xz = across(force[:, 864:866], (1, 0, 1))
    back_yz = across(low_z[:, :, 2], (0, 1, 1))
    back_xyz = across(force[:, 866:867], (1, 1, 1))

    slots = leaving.reshape(6, MIG)
    pos, vel, sent = advance(
        slots.reshape(6 * MIG), force, back_x, back_y, back_xy, back_z, back_xz, back_yz, back_xyz,
        frac, velocity.reshape(3, 512, 128),
    )
    frame = [[0.0] * 8 for _ in range(6)]
    for face in range(6):
        frame[face][face // 2] = BOX[face // 2] * (1.0 if face % 2 == 0 else -1.0)
    alive = (slots >= 0)[:, None, :]
    sent = jnp.where(alive, sent + jnp.array(frame, f32)[:, :, None], 0.0)[:, :6]
    arrivals = jnp.stack(
        [
            across(sent[0], (-1, 0, 0)),
            across(sent[1], (1, 0, 0)),
            across(sent[2], (0, -1, 0)),
            across(sent[3], (0, 1, 0)),
            across(sent[4], (0, 0, -1)),
            across(sent[5], (0, 0, 1)),
        ],
        axis=1,
    ).reshape(6, ARRIVE)
    shape = (3, 1, 1, 1, HOME + ARRIVE)
    new_position = jnp.concatenate([pos.reshape(3, HOME), arrivals[:3]], axis=1).reshape(shape)
    new_velocity = jnp.concatenate([vel.reshape(3, HOME), arrivals[3:]], axis=1).reshape(shape)
    return (new_position, new_velocity)


def solution(mesh):
    cells = P("gx", "gy", "gz", None)
    lists = P("gx", "gy", "gz", None, None)
    vectors = P(None, "gx", "gy", "gz", None)
    return jax.shard_map(
        body,
        mesh=mesh,
        in_specs=(vectors, vectors, cells, cells, P(), lists, lists),
        out_specs=(vectors, vectors),
        check_vma=False,
    )
```

```python
import math
import jax
import jax.numpy as jnp
from jax import lax
from jax.experimental import pallas as pl
from jax.experimental.pallas import tpu as pltpu
from jax.sharding import PartitionSpec as P

CELLS = (16, 2, 16)
MIG = 128
HOME = 65536
ARRIVE = 768
STEP = 0.03
KICK = 0.03 / 144.0
BOX = (64.0, 4.0, 32.0)
C = 872
TILES = 1024
SPAN = (4.0, 2.0, 2.0)
CUTOFF2 = 1.21
NEAR2 = 1.2105
SIGMA2 = 0.2209
FLOOR2 = 0.1764
EDGE_C = (SIGMA2 / CUTOFF2) ** 3
LJ_EDGE = 24.0 * EDGE_C * (2.0 * EDGE_C - 1.0) / CUTOFF2
LJ_A = 48.0 * SIGMA2**6
LJ_B = 24.0 * SIGMA2**3
COULOMB = 138.935458 / 2.5
INV_CUT3 = 1.0 / 1.331
UNROLL = 16
ROWS = 16
LIST = 1152
ITEMS = TILES * 128 // ROWS + 16 * UNROLL
f32 = jnp.float32
bf16 = jnp.bfloat16


def split3(x):
    hi = x.astype(bf16)
    rest = x - hi.astype(f32)
    mid = rest.astype(bf16)
    low = (rest - mid.astype(f32)).astype(bf16)
    return hi, mid, low


def fold8(x):
    return sum((x[8 * m:8 * m + 8] for m in range(1, ROWS // 8)), x[0:8])


def dot_nt(a, b):
    return lax.dot_general(a, b, (((1,), (1,)), ((), ())), preferred_element_type=f32)


def force_kernel(lists, frac, charge, kind, gx, gy, gxy, gz, gyz, gxz, gxyz, same, table,
                 home_out, rx, ry, rxy, rz, ryz, rxz, rxyz, corner, fields, near, dist, rank, half, offs, cnt, ax0, ax1, ax2, bx0, bx1, bx2, counts, at_tile, at_row, spread, picked, depth, eps, pulls, compact, compact2, sem):
    zero = jnp.zeros((8, 128), f32)
    acc_a, acc_b = (ax0, ax1, ax2), (bx0, bx1, bx2)

    sub8 = lax.broadcasted_iota(jnp.int32, (8, 128), 0)
    corner[...] = jnp.zeros((5, 8, 128), f32)
    corner[:, 0:2, :] = gxz[...]
    corner[:, 2:3, :] = gxyz[...]

    def load(values, first, k, cells):
        to = pl.multiple_of(first + 8 * k, 8)
        for m in range(8):
            fields[pl.ds(pl.multiple_of(8 * to + 8 * m, 8), 8), :] = zero
        for acc in acc_a + acc_b:
            for m in range(8):
                acc[pl.ds(pl.multiple_of(8 * to + 8 * m, 8), 8), :] = zero
        for f, r in enumerate(values):
            put = r + cells[f].astype(f32) * SPAN[f] if f < 3 else r
            fields[pl.ds(8 * to + f, 8, stride=8), :] = put
            if f < 3:
                s = SPAN[f] - r
                near[pl.ds(pl.multiple_of(3 * f * C + to, 8), 8), :] = r * r
                near[pl.ds(pl.multiple_of((3 * f + 1) * C + to, 8), 8), :] = zero
                near[pl.ds(pl.multiple_of((3 * f + 2) * C + to, 8), 8), :] = s * s

    def load_home(k, _):
        rows = pl.ds(pl.multiple_of(8 * k, 8), 8)
        c = 8 * k + sub8
        load(bead_values(frac, charge, kind, rows), 0, k, (c >> 5, (c >> 4) & 1, c & 15))
        return 0
    lax.fori_loop(0, 64, load_home, 0)
    high = jnp.full((8, 128), 16, jnp.int32)
    two = jnp.full((8, 128), 2, jnp.int32)
    for src, first, count, cells in (
        (gx, 512, 32, lambda c: (high, c >> 4, c & 15)),
        (gy, 544, 256, lambda c: (c >> 4, two, c & 15)),
        (gxy, 800, 16, lambda c: (high, two, c)),
        (gz, 816, 32, lambda c: (c >> 1, c & 1, high)),
        (gyz, 848, 16, lambda c: (c, two, high)),
        (corner, 864, 8, lambda c: (high, c, high)),
    ):
        def load_ghost(k, _, src=src, first=first, cells=cells):
            rows = pl.ds(pl.multiple_of(8 * k, 8), 8)
            load([src[f, rows, :] for f in range(5)], first, k, cells(8 * k + sub8))
            return 0
        lax.fori_loop(0, count // 8, load_ghost, 0)

    n_live = lists[5 * LIST]

    def stage(k, _):
        for m in range(8):
            t = 8 * k + m
            s = (near[pl.ds(lists[2 * LIST + t], 1), :] + near[pl.ds(lists[3 * LIST + t], 1), :]
                 + near[pl.ds(lists[4 * LIST + t], 1), :])
            dist[pl.ds(8 * k + m, 1), :] = s
        return 0
    lax.fori_loop(0, (n_live + 7) // 8, stage, 0)

    below = (lax.broadcasted_iota(jnp.int32, (128, 128), 0)
             < lax.broadcasted_iota(jnp.int32, (128, 128), 1)).astype(f32).astype(bf16)
    row_id = lax.broadcasted_iota(jnp.int32, (128, 128), 0)
    ones = jnp.ones((16, 128), bf16)
    diagonal = row_id == lax.broadcasted_iota(jnp.int32, (128, 128), 1)
    for g in range(TILES // 128):
        keep = (dist[128 * g:128 * g + 128, :] < NEAR2) & (row_id + 128 * g < n_live)
        hot = jnp.where(keep, 1.0, 0.0).astype(bf16)
        before = jnp.dot(hot, below, preferred_element_type=f32)
        rank[128 * g:128 * g + 128, :] = jnp.where(keep, before, -1.0)
        cnt[g:g + 1, :] = dot_nt(ones, hot)[0:1].astype(jnp.int32)
        column = jnp.sum(jnp.where(diagonal, same[g:g + 1, :], 0.0), axis=1, keepdims=True)
        half[128 * g:128 * g + 128, :] = jnp.broadcast_to(column, (128, 128))
    rank[TILES:LIST, :] = jnp.full((LIST - TILES, 128), -1.0, f32)
    half[TILES:LIST, :] = jnp.zeros((LIST - TILES, 128), f32)
    cnt[TILES // 128:, :] = jnp.zeros((8, 128), jnp.int32)
    for g in range(LIST // 128):
        pltpu.make_async_copy(cnt.at[g], counts.at[pl.ds(128 * g, 128)], sem.at[g]).start()
    offs[...] = lax.broadcasted_iota(jnp.int32, (128, 128), 0).astype(f32)
    for g in range(LIST // 128):
        pltpu.make_async_copy(cnt.at[g], counts.at[pl.ds(128 * g, 128)], sem.at[g]).wait()

    kinds = lax.broadcasted_iota(jnp.int32, (24, 128), 0).astype(f32)
    U = UNROLL

    wr = lax.broadcasted_iota(jnp.int32, (24, 128), 0)
    spread[...] = jnp.zeros((48, 768), f32)
    for f in range(4):
        spread[0:24, 128 * f:128 * f + 128] = jnp.where((wr & 7) == f, 1.0, 0.0)
    t_hi, t_mid, _ = split3(table[0:24, :])
    spread[24:48, 512:640] = t_hi.astype(f32)
    spread[24:48, 640:768] = t_mid.astype(f32)
    weights = spread[...].astype(bf16)

    def decode(n, t, off):
        for u in range(U):
            at_tile[n * U + u] = t
            at_row[n * U + u] = off
            last = off + ROWS >= counts[t]
            t = jnp.where(last, t + 1, t)
            off = jnp.where(last, 0, off + ROWS)
        return t, off

    def chosen(t, off):
        return rank[pl.ds(t, ROWS, stride=0), :] == offs[pl.ds(pl.multiple_of(off, 8), ROWS), :]

    def select(n):
        for u in range(U):
            t, off = at_tile[n * U + u], at_row[n * U + u]
            i = lists[t]
            hot = jnp.where(chosen(t, off), 1.0, 0.0).astype(bf16)
            d = fields[pl.ds(pl.multiple_of(i, 8), 8), :]
            hi = d.astype(bf16).astype(f32)
            mid = (d - hi).astype(bf16).astype(f32)
            kind = jnp.where(fields[pl.ds(i + 4, 24, stride=0), :] == kinds, 1.0, 0.0)
            rows = jnp.concatenate([hi, mid, d - hi - mid, kind], axis=0)
            compact[ROWS * u:ROWS * u + ROWS, :] = dot_nt(hot, rows.astype(bf16)).astype(bf16)

    def well(n):
        c = compact[...]
        d = jnp.dot(c, weights[:, 512:], preferred_element_type=f32)
        depth[...] = d[:, :128] + d[:, 128:]
        compact2[...] = c

    def widen(n):
        picked[...] = jnp.dot(compact2[...], weights[:, :512], preferred_element_type=f32)

    def gather(n):
        for u in range(U):
            j = lists[LIST + at_tile[n * U + u]]
            kb = fields[pl.ds(j + 4, 8, stride=0), :].astype(jnp.int32)
            at = slice(ROWS * u, ROWS * u + ROWS)
            eps[at, :] = jnp.take_along_axis(depth[at, :], jnp.concatenate([kb] * (ROWS // 8), axis=0), axis=1)

    def interact(n):
        for u in range(U):
            t = at_tile[n * U + u]
            j = lists[LIST + t]
            at = slice(ROWS * u, ROWS * u + ROWS)
            ds = [picked[at, 128 * ax:128 * ax + 128] - fields[pl.ds(j + ax, ROWS, stride=0), :] for ax in range(3)]
            qb = fields[pl.ds(j + 3, ROWS, stride=0), :]
            dx, dy, dz = ds
            r2 = dx * dx + dy * dy + dz * dz
            s2 = jnp.maximum(r2, FLOOR2)
            y = lax.rsqrt(s2)
            v = y * y
            v3 = v * v * v
            lj = (v3 - LJ_B / LJ_A) * (v3 * v) - LJ_EDGE / LJ_A
            g = eps[at, :] * lj + (picked[at, 384:512] * qb) * (v * y - INV_CUT3)
            g = jnp.where(r2 < CUTOFF2, g * half[pl.ds(t, ROWS, stride=0), :], 0.0)
            b_rows = pl.ds(pl.multiple_of(j, 8), 8)
            for f in range(3):
                ws = g * ds[f]
                pulls[at, 128 * f:128 * f + 128] = ws
                acc_b[f][b_rows, :] = acc_b[f][b_rows, :] + fold8(ws)

    def gain(n):
        for u in range(U):
            t, off = at_tile[n * U + u], at_row[n * U + u]
            at = slice(ROWS * u, ROWS * u + ROWS)
            sel = chosen(t, off)
            a_rows = pl.ds(pl.multiple_of(lists[t], 8), 8)
            for f in range(3):
                row = jnp.sum(pulls[at, 128 * f:128 * f + 128], axis=1, keepdims=True)
                acc_a[f][a_rows, :] = acc_a[f][a_rows, :] + fold8(jnp.where(sel, row, 0.0))

    for ref in (picked, depth, eps, pulls, compact, compact2):
        ref[...] = jnp.zeros(ref.shape, ref.dtype)
    for u in range(5 * U):
        at_tile[u] = TILES
        at_row[u] = 0

    def work(state):
        n, t, off = state
        t, off = decode(n + 5, t, off)
        gain(n)
        interact(n + 1)
        gather(n + 2)
        widen(n + 2)
        well(n + 3)
        select(n + 4)
        return n + 1, t, off

    lax.while_loop(lambda s: (s[0] < 5) | (at_tile[s[0] * U] < n_live), work, (n_live * 0, n_live * 0, n_live * 0))

    def folded(f, row):
        a = acc_a[f][pl.ds(8 * row, 8, stride=8), :]
        b = acc_b[f][pl.ds(8 * row, 8, stride=8), :]
        for m in range(1, 8):
            a = a + acc_a[f][pl.ds(8 * row + m, 8, stride=8), :]
            b = b + acc_b[f][pl.ds(8 * row + m, 8, stride=8), :]
        return a - b

    for f in range(3):
        for to, first, count in (
            (home_out, 0, 512), (rx, 512, 32), (ry, 544, 256), (rxy, 800, 16), (rz, 816, 32), (ryz, 848, 16),
        ):
            def give(k, _, f=f, to=to, first=first):
                to[f, pl.ds(pl.multiple_of(8 * k, 8), 8), :] = folded(f, first + 8 * k)
                return 0
            lax.fori_loop(0, count // 8, give, 0)
        last = folded(f, 864)
        rxz[f] = last[0:2]
        rxyz[f] = last[2:3]


def bead_values(frac, charge, kind, rows):
    values = [frac[f, rows, :] * SPAN[f] for f in range(3)]
    return values + [charge[rows, :] * math.sqrt(COULOMB), (kind[rows, :] + 1).astype(f32)]


GHOSTS = ((32, (1, 0, 0)), (256, (0, 1, 0)), (16, (1, 1, 0)), (32, (0, 0, 1)), (16, (0, 1, 1)), (2, (1, 0, 1)), (1, (1, 1, 1)))


def forces(lists, *arrays):
    vm = pl.BlockSpec(memory_space=pltpu.VMEM)
    sm = pl.BlockSpec(memory_space=pltpu.SMEM)
    return pl.pallas_call(
        force_kernel,
        out_shape=[jax.ShapeDtypeStruct((3, n, 128), f32) for n in (512,) + tuple(n for n, _ in GHOSTS)],
        in_specs=[sm] + [vm] * len(arrays),
        out_specs=[vm] * 8,
        scratch_shapes=[
            pltpu.VMEM((5, 8, 128), f32),
            pltpu.VMEM((8 * C, 128), f32),
            pltpu.VMEM((9 * C, 128), f32),
            pltpu.VMEM((TILES, 128), f32),
            pltpu.VMEM((LIST, 128), f32),
            pltpu.VMEM((LIST, 128), f32),
            pltpu.VMEM((128, 128), f32),
            pltpu.VMEM((16, 128), jnp.int32),
            *[pltpu.VMEM((8 * C, 128), f32)] * 6,
            pltpu.SMEM((LIST,), jnp.int32),
            pltpu.SMEM((ITEMS,), jnp.int32),
            pltpu.SMEM((ITEMS,), jnp.int32),
            pltpu.VMEM((48, 768), f32),
            pltpu.VMEM((ROWS * UNROLL, 512), f32),
            pltpu.VMEM((ROWS * UNROLL, 128), f32),
            pltpu.VMEM((ROWS * UNROLL, 128), f32),
            pltpu.VMEM((ROWS * UNROLL, 384), f32),
            pltpu.VMEM((ROWS * UNROLL, 48), bf16),
            pltpu.VMEM((ROWS * UNROLL, 48), bf16),
            pltpu.SemaphoreType.DMA((LIST // 128,)),
        ],
        compiler_params=pltpu.CompilerParams(vmem_limit_bytes=56 * 2**20),
        name="pair_forces",
    )(lists, *arrays)


def pack_kernel(pairs, frac, charge, kind, lists, same, sx, sy, sxy, sz, syz, sxz, sxyz, beads):
    def fill(k, _):
        rows = pl.ds(pl.multiple_of(8 * k, 8), 8)
        for f, value in enumerate(bead_values(frac, charge, kind, rows)):
            beads[f, rows, :] = value
        return 0
    lax.fori_loop(0, 64, fill, 0, unroll=4)
    for f in range(5):
        sx[f] = beads[f, 0:32, :]
        for k in range(16):
            sy[f, 16 * k:16 * k + 16, :] = beads[f, 32 * k:32 * k + 16, :]
            syz[f, k:k + 1, :] = beads[f, 32 * k:32 * k + 1, :]
        sxy[f] = beads[f, 0:16, :]
        for k in range(32):
            sz[f, k:k + 1, :] = beads[f, 16 * k:16 * k + 1, :]
        sxz[f, 0:1, :] = beads[f, 0:1, :]
        sxz[f, 1:2, :] = beads[f, 16:17, :]
        sxyz[f] = beads[f, 0:1, :]

    first, second = pairs[0], pairs[1]
    lists[...] = jnp.zeros((48, 128), jnp.int32)
    count = jnp.sum((first >= 0).astype(f32), axis=(0, 1), keepdims=True)
    lists[45:46, :] = jnp.broadcast_to(count, (1, 128)).astype(jnp.int32)
    i, a = placed(jnp.maximum(first, 0))
    j, b = placed(jnp.maximum(second, 0))
    lists[0:8, :] = 8 * i
    lists[9:17, :] = 8 * j
    for f in range(3):
        lists[18 + 9 * f:26 + 9 * f, :] = (3 * f + b[f] - a[f] + 1) * C + i
    same[...] = jnp.where(first == second, 0.5, 1.0)


def placed(index):
    home, on_x, on_y = index < 512, index < 544, index < 816
    y, z = index - 544, index - 816
    zx = (z * 171) >> 9
    zy = z - 3 * zx
    bx = jnp.where(home, index >> 5, jnp.where(on_x, 16, jnp.where(on_y, y >> 4, zx)))
    by = jnp.where(home, (index >> 4) & 1, jnp.where(on_x, ((index - 512) >> 4) & 1, jnp.where(on_y, 2, zy)))
    bz = jnp.where(on_y, index & 15, 16)
    lower = jnp.where(zx < 16, 816 + 2 * zx + zy, 864 + zy)
    upper = jnp.where(zx < 16, 848 + zx, 866)
    row = jnp.where(on_y, index, jnp.where(zy < 2, lower, upper))
    return row, (bx, by, bz)


def pack(*arrays):
    vm = pl.BlockSpec(memory_space=pltpu.VMEM)
    return pl.pallas_call(
        pack_kernel,
        out_shape=[jax.ShapeDtypeStruct((48, 128), jnp.int32), jax.ShapeDtypeStruct((8, 128), f32)]
        + [jax.ShapeDtypeStruct((5, n, 128), f32) for n, _ in GHOSTS],
        in_specs=[vm] * len(arrays),
        out_specs=[vm] * 9,
        scratch_shapes=[pltpu.VMEM((5, 512, 128), f32)],
        compiler_params=pltpu.CompilerParams(vmem_limit_bytes=40 * 2**20),
        name="pack",
    )(*arrays)


def keep_kernel(leaving, keep):
    lane = lax.broadcasted_iota(jnp.int32, (1, 128), 1)
    keep[...] = jnp.ones((512, 128), f32)

    def drop(k, _):
        for u in range(8):
            slot = leaving[8 * k + u]
            at = jnp.maximum(slot, 0)
            row = pl.ds(at >> 7, 1)
            keep[row, :] = jnp.where(lane == jnp.where(slot >= 0, at & 127, -1), 0.0, keep[row, :])
        return 0
    lax.fori_loop(0, 6 * MIG // 8, drop, 0)


def kept(leaving):
    return pl.pallas_call(
        keep_kernel,
        out_shape=jax.ShapeDtypeStruct((512, 128), f32),
        in_specs=[pl.BlockSpec(memory_space=pltpu.SMEM)],
        out_specs=pl.BlockSpec(memory_space=pltpu.VMEM),
        cost_estimate=pl.CostEstimate(flops=10**6, bytes_accessed=262144, transcendentals=0),
        name="kept",
    )(leaving)


def advance_kernel(leaving, force, bx, by, bxy, bz, byz, bxz, bxyz, keep, fraction, velocity,
                   pos, vel, s0, s1, s2, s3, s4, s5, total, beads):
    for f in range(3):
        total[f] = force[f]
        total[f, 0:32, :] = total[f, 0:32, :] + bx[f]
        for k in range(16):
            total[f, 32 * k:32 * k + 16, :] = total[f, 32 * k:32 * k + 16, :] + by[f, 16 * k:16 * k + 16, :]
        total[f, 0:16, :] = total[f, 0:16, :] + bxy[f]
        for k in range(32):
            total[f, 16 * k:16 * k + 1, :] = total[f, 16 * k:16 * k + 1, :] + bz[f, k:k + 1, :]
        for k in range(16):
            total[f, 32 * k:32 * k + 1, :] = total[f, 32 * k:32 * k + 1, :] + byz[f, k:k + 1, :]
        for k in range(2):
            total[f, 16 * k:16 * k + 1, :] = total[f, 16 * k:16 * k + 1, :] + bxz[f, k:k + 1, :]
        total[f, 0:1, :] = total[f, 0:1, :] + bxyz[f]

    sub = lax.broadcasted_iota(jnp.int32, (8, 128), 0)
    lane = lax.broadcasted_iota(jnp.int32, (8, 128), 1)

    def move(k, _):
        rows = pl.ds(pl.multiple_of(8 * k, 8), 8)
        cluster = 8 * k + sub
        cells = (cluster >> 5, (cluster >> 4) & 1, cluster & 15)
        for f in range(3):
            half = velocity[f, rows, :] + KICK * total[f, rows, :]
            place = (cells[f].astype(f32) + fraction[f, rows, :]) * SPAN[f] + STEP * half
            beads[pl.ds(64 * k + f, 8, stride=8), :] = place
            beads[pl.ds(64 * k + 3 + f, 8, stride=8), :] = half
            pos[f, rows, :] = place * keep[rows, :]
            vel[f, rows, :] = half * keep[rows, :]
        return 0
    lax.fori_loop(0, 64, move, 0, unroll=2)

    for face, sent in enumerate((s0, s1, s2, s3, s4, s5)):
        span = BOX[face // 2] if face % 2 == 0 else -BOX[face // 2]
        shift = jnp.where(sub == face // 2, span, 0.0)

        def pick(k, taken, face=face, shift=shift):
            for u in range(8):
                m = 8 * k + u
                slot = leaving[face * MIG + m]
                at = jnp.maximum(slot, 0)
                row = beads[pl.ds(pl.multiple_of((at >> 7) * 8, 8), 8), :]
                row = pltpu.roll(row, (m - at) & 127, 1) + shift
                taken = jnp.where(lane == jnp.where(slot >= 0, m, -1), row, taken)
            return taken
        taken = lax.fori_loop(0, MIG // 8, pick, jnp.zeros((8, 128), f32), unroll=4)
        sent[...] = taken[0:6]


def advance(leaving, *arrays):
    vm = pl.BlockSpec(memory_space=pltpu.VMEM)
    sm = pl.BlockSpec(memory_space=pltpu.SMEM)
    return pl.pallas_call(
        advance_kernel,
        out_shape=[jax.ShapeDtypeStruct((3, 512, 128), f32)] * 2 + [jax.ShapeDtypeStruct((6, 128), f32)] * 6,
        in_specs=[sm] + [vm] * len(arrays),
        out_specs=[vm] * 8,
        scratch_shapes=[pltpu.VMEM((3, 512, 128), f32), pltpu.VMEM((4096, 128), f32)],
        compiler_params=pltpu.CompilerParams(vmem_limit_bytes=40 * 2**20),
        name="advance",
    )(leaving, *arrays)


def across(block, step):
    names = tuple(n for n, s in zip(("gx", "gy", "gz"), step) if s)
    steps = [s for s in step if s]
    sizes = [lax.axis_size(n) for n in names]
    pairs = []
    for flat in range(math.prod(sizes)):
        rest, source = flat, []
        for size in reversed(sizes):
            source.insert(0, rest % size)
            rest //= size
        target = 0
        inside = True
        for name, size, at, s in zip(names, sizes, source, steps):
            to = at + s
            if name == "gz" and not 0 <= to < size:
                inside = False
            target = target * size + to % size
        if inside:
            pairs.append((flat, target))
    return lax.ppermute(block, names if len(names) > 1 else names[0], pairs)


def body(fraction, velocity, charge, bead_type, well_depth, tile_list, leaving):
    frac = fraction.reshape(3, 512, 128)
    charges = charge.reshape(512, 128)
    kinds = bead_type.reshape(512, 128)
    slots = leaving.reshape(6 * MIG)
    pairs = tile_list.reshape(TILES, 2).T.reshape(2, 8, 128)
    table = jnp.pad((0.5 * LJ_A) * (well_depth + well_depth.T), ((1, 109), (1, 109)))
    lists, same, *faces = pack(pairs, frac, charges, kinds)
    ghosts = [across(face, tuple(-s for s in step)) for face, (_, step) in zip(faces, GHOSTS)]
    keep = kept(slots)
    force, *returned = forces(lists.reshape(6144), frac, charges, kinds, *ghosts, same, table)
    back = [across(face, step) for face, (_, step) in zip(returned, GHOSTS)]
    pos, vel, *sent = advance(slots, force, *back, keep, frac, velocity.reshape(3, 512, 128))
    steps = ((-1, 0, 0), (1, 0, 0), (0, -1, 0), (0, 1, 0), (0, 0, -1), (0, 0, 1))
    arrivals = [across(face, step) for face, step in zip(sent, steps)]
    shape = (3, 1, 1, 1, HOME + ARRIVE)
    new_position = jnp.concatenate([pos.reshape(3, HOME)] + [a[:3] for a in arrivals], axis=1).reshape(shape)
    new_velocity = jnp.concatenate([vel.reshape(3, HOME)] + [a[3:] for a in arrivals], axis=1).reshape(shape)
    return (new_position, new_velocity)


def solution(mesh):
    cells = P("gx", "gy", "gz", None)
    lists = P("gx", "gy", "gz", None, None)
    vectors = P(None, "gx", "gy", "gz", None)
    return jax.shard_map(
        body,
        mesh=mesh,
        in_specs=(vectors, vectors, cells, cells, P(), lists, lists),
        out_specs=(vectors, vectors),
        check_vma=False,
    )
```

```python
import math
import jax
import jax.numpy as jnp
from jax import lax
from jax.experimental import pallas as pl
from jax.experimental.pallas import tpu as pltpu
from jax.sharding import PartitionSpec as P

CELLS = (16, 2, 16)
MIG = 128
HOME = 65536
ARRIVE = 768
STEP = 0.03
KICK = 0.03 / 144.0
BOX = (64.0, 4.0, 32.0)
C = 872
TILES = 1024
SPAN = (4.0, 2.0, 2.0)
CUTOFF2 = 1.21
NEAR2 = 1.2105
SIGMA2 = 0.2209
FLOOR2 = 0.1764
EDGE_C = (SIGMA2 / CUTOFF2) ** 3
LJ_EDGE = 24.0 * EDGE_C * (2.0 * EDGE_C - 1.0) / CUTOFF2
LJ_A = 48.0 * SIGMA2**6
LJ_B = 24.0 * SIGMA2**3
COULOMB = 138.935458 / 2.5
INV_CUT3 = 1.0 / 1.331
UNROLL = 28
ROWS = 16
LIST = 1280
ITEMS = TILES * 128 // ROWS + 16 * UNROLL
f32 = jnp.float32
bf16 = jnp.bfloat16


def split3(x):
    hi = x.astype(bf16)
    rest = x - hi.astype(f32)
    mid = rest.astype(bf16)
    low = (rest - mid.astype(f32)).astype(bf16)
    return hi, mid, low


def fold8(x):
    return sum((x[8 * m:8 * m + 8] for m in range(1, ROWS // 8)), x[0:8])


def dot_nt(a, b):
    return lax.dot_general(a, b, (((1,), (1,)), ((), ())), preferred_element_type=f32)


def force_kernel(lists, frac, charge, kind, gx, gy, gxy, gz, gyz, gxz, gxyz, same, table, keep,
                 home_out, rx, ry, rxy, rz, ryz, rxz, rxyz, corner, fields, near, dist, rank, half, offs, cnt, ax0, ax1, ax2, bx0, bx1, bx2, counts, at_tile, at_row, spread, picked, depth, eps, pulls, compact, compact2, sem):
    zero = jnp.zeros((8, 128), f32)
    acc_a, acc_b = (ax0, ax1, ax2), (bx0, bx1, bx2)

    sub8 = lax.broadcasted_iota(jnp.int32, (8, 128), 0)
    corner[...] = jnp.zeros((5, 8, 128), f32)
    corner[:, 0:2, :] = gxz[...]
    corner[:, 2:3, :] = gxyz[...]

    def load(values, first, k, cells):
        to = pl.multiple_of(first + 8 * k, 8)
        for m in range(8):
            fields[pl.ds(pl.multiple_of(8 * to + 8 * m, 8), 8), :] = zero
        for acc in acc_a + acc_b:
            for m in range(8):
                acc[pl.ds(pl.multiple_of(8 * to + 8 * m, 8), 8), :] = zero
        for f, r in enumerate(values):
            put = r + cells[f].astype(f32) * SPAN[f] if f < 3 else r
            fields[pl.ds(8 * to + f, 8, stride=8), :] = put
            if f < 3:
                s = SPAN[f] - r
                near[pl.ds(pl.multiple_of(3 * f * C + to, 8), 8), :] = r * r
                near[pl.ds(pl.multiple_of((3 * f + 1) * C + to, 8), 8), :] = zero
                near[pl.ds(pl.multiple_of((3 * f + 2) * C + to, 8), 8), :] = s * s

    def load_home(k, _):
        rows = pl.ds(pl.multiple_of(8 * k, 8), 8)
        c = 8 * k + sub8
        load(bead_values(frac, charge, kind, rows), 0, k, (c >> 5, (c >> 4) & 1, c & 15))
        return 0
    lax.fori_loop(0, 64, load_home, 0, unroll=2)
    high = jnp.full((8, 128), 16, jnp.int32)
    two = jnp.full((8, 128), 2, jnp.int32)
    for src, first, count, cells in (
        (gx, 512, 32, lambda c: (high, c >> 4, c & 15)),
        (gy, 544, 256, lambda c: (c >> 4, two, c & 15)),
        (gxy, 800, 16, lambda c: (high, two, c)),
        (gz, 816, 32, lambda c: (c >> 1, c & 1, high)),
        (gyz, 848, 16, lambda c: (c, two, high)),
        (corner, 864, 8, lambda c: (high, c, high)),
    ):
        def load_ghost(k, _, src=src, first=first, cells=cells):
            rows = pl.ds(pl.multiple_of(8 * k, 8), 8)
            load([src[f, rows, :] for f in range(5)], first, k, cells(8 * k + sub8))
            return 0
        lax.fori_loop(0, count // 8, load_ghost, 0)

    n_live = lists[5 * LIST]

    def stage(k, _):
        for m in range(32):
            t = 32 * k + m
            s = (near[pl.ds(lists[2 * LIST + t], 1), :] + near[pl.ds(lists[3 * LIST + t], 1), :]
                 + near[pl.ds(lists[4 * LIST + t], 1), :])
            dist[pl.ds(t, 1), :] = s
        return 0
    lax.fori_loop(0, (n_live + 31) // 32, stage, 0)

    below = (lax.broadcasted_iota(jnp.int32, (128, 128), 0)
             < lax.broadcasted_iota(jnp.int32, (128, 128), 1)).astype(f32).astype(bf16)
    row_id = lax.broadcasted_iota(jnp.int32, (128, 128), 0)
    ones = jnp.ones((16, 128), bf16)
    diagonal = row_id == lax.broadcasted_iota(jnp.int32, (128, 128), 1)
    for g in range(TILES // 128):
        keep = (dist[128 * g:128 * g + 128, :] < NEAR2) & (row_id + 128 * g < n_live)
        hot = jnp.where(keep, 1.0, 0.0).astype(bf16)
        before = jnp.dot(hot, below, preferred_element_type=f32)
        rank[128 * g:128 * g + 128, :] = jnp.where(keep, before, -1.0)
        cnt[g:g + 1, :] = dot_nt(ones, hot)[0:1].astype(jnp.int32)
        column = jnp.sum(jnp.where(diagonal, same[g:g + 1, :], 0.0), axis=1, keepdims=True)
        half[128 * g:128 * g + 128, :] = jnp.broadcast_to(column, (128, 128))
    rank[TILES:LIST, :] = jnp.full((LIST - TILES, 128), -1.0, f32)
    half[TILES:LIST, :] = jnp.zeros((LIST - TILES, 128), f32)
    cnt[TILES // 128:, :] = jnp.zeros((8, 128), jnp.int32)
    for g in range(LIST // 128):
        pltpu.make_async_copy(cnt.at[g], counts.at[pl.ds(128 * g, 128)], sem.at[g]).start()
    offs[...] = lax.broadcasted_iota(jnp.int32, (128, 128), 0).astype(f32)
    for g in range(LIST // 128):
        pltpu.make_async_copy(cnt.at[g], counts.at[pl.ds(128 * g, 128)], sem.at[g]).wait()

    kinds = lax.broadcasted_iota(jnp.int32, (24, 128), 0).astype(f32)
    U = UNROLL

    wr = lax.broadcasted_iota(jnp.int32, (24, 128), 0)
    spread[...] = jnp.zeros((48, 768), f32)
    for f in range(4):
        spread[0:24, 128 * f:128 * f + 128] = jnp.where((wr & 7) == f, 1.0, 0.0)
    t_hi, t_mid, _ = split3(table[0:24, :])
    spread[24:48, 512:640] = t_hi.astype(f32)
    spread[24:48, 640:768] = t_mid.astype(f32)
    weights = spread[...].astype(bf16)

    def decode(n, t, off):
        for u in range(U):
            at_tile[n * U + u] = t
            at_row[n * U + u] = off
            last = off + ROWS >= counts[t]
            t = jnp.where(last, t + 1, t)
            off = jnp.where(last, 0, off + ROWS)
        return t, off

    def chosen(t, off):
        return rank[pl.ds(t, ROWS, stride=0), :] == offs[pl.ds(pl.multiple_of(off, 8), ROWS), :]

    def select(n):
        for u in range(U):
            t, off = at_tile[n * U + u], at_row[n * U + u]
            i = lists[t]
            hot = jnp.where(chosen(t, off), 1.0, 0.0).astype(bf16)
            d = fields[pl.ds(pl.multiple_of(i, 8), 8), :]
            hi = d.astype(bf16).astype(f32)
            mid = (d - hi).astype(bf16).astype(f32)
            kind = jnp.where(fields[pl.ds(i + 4, 24, stride=0), :] == kinds, 1.0, 0.0)
            rows = jnp.concatenate([hi, mid, d - hi - mid, kind], axis=0)
            compact[ROWS * u:ROWS * u + ROWS, :] = dot_nt(hot, rows.astype(bf16)).astype(bf16)

    def well(n):
        c = compact[...]
        d = jnp.dot(c, weights[:, 512:], preferred_element_type=f32)
        depth[...] = d[:, :128] + d[:, 128:]
        compact2[...] = c

    def widen(n):
        picked[...] = jnp.dot(compact2[...], weights[:, :512], preferred_element_type=f32)

    def gather(n):
        for u in range(U):
            j = lists[LIST + at_tile[n * U + u]]
            kb = fields[pl.ds(j + 4, 8, stride=0), :].astype(jnp.int32)
            at = slice(ROWS * u, ROWS * u + ROWS)
            eps[at, :] = jnp.take_along_axis(depth[at, :], jnp.concatenate([kb] * (ROWS // 8), axis=0), axis=1)

    def interact(n):
        for u in range(U):
            t = at_tile[n * U + u]
            j = lists[LIST + t]
            at = slice(ROWS * u, ROWS * u + ROWS)
            ds = [picked[at, 128 * ax:128 * ax + 128] - fields[pl.ds(j + ax, ROWS, stride=0), :] for ax in range(3)]
            qb = fields[pl.ds(j + 3, ROWS, stride=0), :]
            dx, dy, dz = ds
            r2 = dx * dx + dy * dy + dz * dz
            s2 = jnp.maximum(r2, FLOOR2)
            y = lax.rsqrt(s2)
            v = y * y
            v3 = v * v * v
            lj = (v3 - LJ_B / LJ_A) * (v3 * v) - LJ_EDGE / LJ_A
            g = eps[at, :] * lj + (picked[at, 384:512] * qb) * (v * y - INV_CUT3)
            g = jnp.where(r2 < CUTOFF2, g * half[pl.ds(t, ROWS, stride=0), :], 0.0)
            b_rows = pl.ds(pl.multiple_of(j, 8), 8)
            for f in range(3):
                ws = g * ds[f]
                pulls[at, 128 * f:128 * f + 128] = ws
                acc_b[f][b_rows, :] = acc_b[f][b_rows, :] + fold8(ws)

    def gain(n):
        for u in range(U):
            t, off = at_tile[n * U + u], at_row[n * U + u]
            at = slice(ROWS * u, ROWS * u + ROWS)
            sel = chosen(t, off)
            a_rows = pl.ds(pl.multiple_of(lists[t], 8), 8)
            for f in range(3):
                row = jnp.sum(pulls[at, 128 * f:128 * f + 128], axis=1, keepdims=True)
                acc_a[f][a_rows, :] = acc_a[f][a_rows, :] + fold8(jnp.where(sel, row, 0.0))

    for ref in (picked, depth, eps, pulls, compact, compact2):
        ref[...] = jnp.zeros(ref.shape, ref.dtype)
    for u in range(5 * U):
        at_tile[u] = TILES
        at_row[u] = 0

    def work(state):
        n, t, off = state
        t, off = decode(n + 5, t, off)
        gain(n)
        interact(n + 1)
        gather(n + 2)
        widen(n + 2)
        well(n + 3)
        select(n + 4)
        return n + 1, t, off

    lax.while_loop(lambda s: (s[0] < 5) | (at_tile[s[0] * U] < n_live), work, (n_live * 0, n_live * 0, n_live * 0))

    def folded(f, row):
        a = acc_a[f][pl.ds(8 * row, 8, stride=8), :]
        b = acc_b[f][pl.ds(8 * row, 8, stride=8), :]
        for m in range(1, 8):
            a = a + acc_a[f][pl.ds(8 * row + m, 8, stride=8), :]
            b = b + acc_b[f][pl.ds(8 * row + m, 8, stride=8), :]
        return a - b

    for f in range(3):
        for to, first, count in (
            (home_out, 0, 512), (rx, 512, 32), (ry, 544, 256), (rxy, 800, 16), (rz, 816, 32), (ryz, 848, 16),
        ):
            def give(k, _, f=f, to=to, first=first):
                to[f, pl.ds(pl.multiple_of(8 * k, 8), 8), :] = folded(f, first + 8 * k)
                return 0
            lax.fori_loop(0, count // 8, give, 0, unroll=min(4, count // 8))
        last = folded(f, 864)
        rxz[f] = last[0:2]
        rxyz[f] = last[2:3]


def bead_values(frac, charge, kind, rows):
    values = [frac[f, rows, :] * SPAN[f] for f in range(3)]
    return values + [charge[rows, :] * math.sqrt(COULOMB), (kind[rows, :] + 1).astype(f32)]


GHOSTS = ((32, (1, 0, 0)), (256, (0, 1, 0)), (16, (1, 1, 0)), (32, (0, 0, 1)), (16, (0, 1, 1)), (2, (1, 0, 1)), (1, (1, 1, 1)))


def forces(lists, *arrays):
    vm = pl.BlockSpec(memory_space=pltpu.VMEM)
    sm = pl.BlockSpec(memory_space=pltpu.SMEM)
    return pl.pallas_call(
        force_kernel,
        out_shape=[jax.ShapeDtypeStruct((3, n, 128), f32) for n in (512,) + tuple(n for n, _ in GHOSTS)],
        in_specs=[sm] + [vm] * (len(arrays) - 1) + [pl.BlockSpec(memory_space=pl.ANY)],
        out_specs=[vm] * 8,
        scratch_shapes=[
            pltpu.VMEM((5, 8, 128), f32),
            pltpu.VMEM((8 * C, 128), f32),
            pltpu.VMEM((9 * C, 128), f32),
            pltpu.VMEM((TILES, 128), f32),
            pltpu.VMEM((LIST, 128), f32),
            pltpu.VMEM((LIST, 128), f32),
            pltpu.VMEM((128, 128), f32),
            pltpu.VMEM((16, 128), jnp.int32),
            *[pltpu.VMEM((8 * C, 128), f32)] * 6,
            pltpu.SMEM((LIST,), jnp.int32),
            pltpu.SMEM((ITEMS,), jnp.int32),
            pltpu.SMEM((ITEMS,), jnp.int32),
            pltpu.VMEM((48, 768), f32),
            pltpu.VMEM((ROWS * UNROLL, 512), f32),
            pltpu.VMEM((ROWS * UNROLL, 128), f32),
            pltpu.VMEM((ROWS * UNROLL, 128), f32),
            pltpu.VMEM((ROWS * UNROLL, 384), f32),
            pltpu.VMEM((ROWS * UNROLL, 48), bf16),
            pltpu.VMEM((ROWS * UNROLL, 48), bf16),
            pltpu.SemaphoreType.DMA((LIST // 128,)),
        ],
        compiler_params=pltpu.CompilerParams(vmem_limit_bytes=56 * 2**20),
        name="pair_forces",
    )(lists, *arrays)


def pack_kernel(pairs, frac, charge, kind, lists, same, sx, sy, sxy, sz, syz, sxz, sxyz, beads):
    def fill(k, _):
        rows = pl.ds(pl.multiple_of(8 * k, 8), 8)
        for f, value in enumerate(bead_values(frac, charge, kind, rows)):
            beads[f, rows, :] = value
        return 0
    lax.fori_loop(0, 64, fill, 0, unroll=4)
    for f in range(5):
        sx[f] = beads[f, 0:32, :]
        for k in range(16):
            sy[f, 16 * k:16 * k + 16, :] = beads[f, 32 * k:32 * k + 16, :]
            syz[f, k:k + 1, :] = beads[f, 32 * k:32 * k + 1, :]
        sxy[f] = beads[f, 0:16, :]
        for k in range(32):
            sz[f, k:k + 1, :] = beads[f, 16 * k:16 * k + 1, :]
        sxz[f, 0:1, :] = beads[f, 0:1, :]
        sxz[f, 1:2, :] = beads[f, 16:17, :]
        sxyz[f] = beads[f, 0:1, :]

    first, second = pairs[0], pairs[1]
    lists[...] = jnp.zeros((56, 128), jnp.int32)
    count = jnp.sum((first >= 0).astype(f32), axis=(0, 1), keepdims=True)
    lists[50:51, :] = jnp.broadcast_to(count, (1, 128)).astype(jnp.int32)
    i, a = placed(jnp.maximum(first, 0))
    j, b = placed(jnp.maximum(second, 0))
    lists[0:8, :] = 8 * i
    lists[10:18, :] = 8 * j
    for f in range(3):
        lists[20 + 10 * f:28 + 10 * f, :] = (3 * f + b[f] - a[f] + 1) * C + i
    same[...] = jnp.where(first == second, 0.5, 1.0)


def placed(index):
    home, on_x, on_y = index < 512, index < 544, index < 816
    y, z = index - 544, index - 816
    zx = (z * 171) >> 9
    zy = z - 3 * zx
    bx = jnp.where(home, index >> 5, jnp.where(on_x, 16, jnp.where(on_y, y >> 4, zx)))
    by = jnp.where(home, (index >> 4) & 1, jnp.where(on_x, ((index - 512) >> 4) & 1, jnp.where(on_y, 2, zy)))
    bz = jnp.where(on_y, index & 15, 16)
    lower = jnp.where(zx < 16, 816 + 2 * zx + zy, 864 + zy)
    upper = jnp.where(zx < 16, 848 + zx, 866)
    row = jnp.where(on_y, index, jnp.where(zy < 2, lower, upper))
    return row, (bx, by, bz)


def pack(*arrays):
    vm = pl.BlockSpec(memory_space=pltpu.VMEM)
    return pl.pallas_call(
        pack_kernel,
        out_shape=[jax.ShapeDtypeStruct((56, 128), jnp.int32), jax.ShapeDtypeStruct((8, 128), f32)]
        + [jax.ShapeDtypeStruct((5, n, 128), f32) for n, _ in GHOSTS],
        in_specs=[vm] * len(arrays),
        out_specs=[vm] * 9,
        scratch_shapes=[pltpu.VMEM((5, 512, 128), f32)],
        compiler_params=pltpu.CompilerParams(vmem_limit_bytes=40 * 2**20),
        name="pack",
    )(*arrays)


def keep_kernel(leaving, keep):
    lane = lax.broadcasted_iota(jnp.int32, (1, 128), 1)
    keep[...] = jnp.ones((512, 128), f32)

    def drop(k, _):
        for u in range(8):
            slot = leaving[8 * k + u]
            at = jnp.maximum(slot, 0)
            row = pl.ds(at >> 7, 1)
            keep[row, :] = jnp.where(lane == jnp.where(slot >= 0, at & 127, -1), 0.0, keep[row, :])
        return 0
    lax.fori_loop(0, 6 * MIG // 8, drop, 0)


def kept(leaving):
    return pl.pallas_call(
        keep_kernel,
        out_shape=jax.ShapeDtypeStruct((512, 128), f32),
        in_specs=[pl.BlockSpec(memory_space=pltpu.SMEM)],
        out_specs=pl.BlockSpec(memory_space=pltpu.VMEM),
        cost_estimate=pl.CostEstimate(flops=10**6, bytes_accessed=262144, transcendentals=0),
        name="kept",
    )(leaving)


def advance_kernel(leaving, force, bx, by, bxy, bz, byz, bxz, bxyz, keep, fraction, velocity,
                   pos, vel, s0, s1, s2, s3, s4, s5, total, beads):
    for f in range(3):
        total[f] = force[f]
        total[f, 0:32, :] = total[f, 0:32, :] + bx[f]
        for k in range(16):
            total[f, 32 * k:32 * k + 16, :] = total[f, 32 * k:32 * k + 16, :] + by[f, 16 * k:16 * k + 16, :]
        total[f, 0:16, :] = total[f, 0:16, :] + bxy[f]
        for k in range(32):
            total[f, 16 * k:16 * k + 1, :] = total[f, 16 * k:16 * k + 1, :] + bz[f, k:k + 1, :]
        for k in range(16):
            total[f, 32 * k:32 * k + 1, :] = total[f, 32 * k:32 * k + 1, :] + byz[f, k:k + 1, :]
        for k in range(2):
            total[f, 16 * k:16 * k + 1, :] = total[f, 16 * k:16 * k + 1, :] + bxz[f, k:k + 1, :]
        total[f, 0:1, :] = total[f, 0:1, :] + bxyz[f]

    sub = lax.broadcasted_iota(jnp.int32, (8, 128), 0)
    lane = lax.broadcasted_iota(jnp.int32, (8, 128), 1)

    def move(k, _):
        rows = pl.ds(pl.multiple_of(8 * k, 8), 8)
        cluster = 8 * k + sub
        cells = (cluster >> 5, (cluster >> 4) & 1, cluster & 15)
        for f in range(3):
            half = velocity[f, rows, :] + KICK * total[f, rows, :]
            place = (cells[f].astype(f32) + fraction[f, rows, :]) * SPAN[f] + STEP * half
            beads[pl.ds(64 * k + f, 8, stride=8), :] = place
            beads[pl.ds(64 * k + 3 + f, 8, stride=8), :] = half
            pos[f, rows, :] = place * keep[rows, :]
            vel[f, rows, :] = half * keep[rows, :]
        return 0
    lax.fori_loop(0, 64, move, 0, unroll=2)

    for face, sent in enumerate((s0, s1, s2, s3, s4, s5)):
        span = BOX[face // 2] if face % 2 == 0 else -BOX[face // 2]
        shift = jnp.where(sub == face // 2, span, 0.0)

        def pick(k, taken, face=face, shift=shift):
            for u in range(8):
                m = 8 * k + u
                slot = leaving[face * MIG + m]
                at = jnp.maximum(slot, 0)
                row = beads[pl.ds(pl.multiple_of((at >> 7) * 8, 8), 8), :]
                row = pltpu.roll(row, (m - at) & 127, 1) + shift
                taken = jnp.where(lane == jnp.where(slot >= 0, m, -1), row, taken)
            return taken
        taken = lax.fori_loop(0, MIG // 8, pick, jnp.zeros((8, 128), f32), unroll=4)
        sent[...] = taken[0:6]


def advance(leaving, *arrays):
    vm = pl.BlockSpec(memory_space=pltpu.VMEM)
    sm = pl.BlockSpec(memory_space=pltpu.SMEM)
    return pl.pallas_call(
        advance_kernel,
        out_shape=[jax.ShapeDtypeStruct((3, 512, 128), f32)] * 2 + [jax.ShapeDtypeStruct((6, 128), f32)] * 6,
        in_specs=[sm] + [vm] * len(arrays),
        out_specs=[vm] * 8,
        scratch_shapes=[pltpu.VMEM((3, 512, 128), f32), pltpu.VMEM((4096, 128), f32)],
        compiler_params=pltpu.CompilerParams(vmem_limit_bytes=40 * 2**20),
        name="advance",
    )(leaving, *arrays)


def across(block, step):
    names = tuple(n for n, s in zip(("gx", "gy", "gz"), step) if s)
    steps = [s for s in step if s]
    sizes = [lax.axis_size(n) for n in names]
    pairs = []
    for flat in range(math.prod(sizes)):
        rest, source = flat, []
        for size in reversed(sizes):
            source.insert(0, rest % size)
            rest //= size
        target = 0
        inside = True
        for name, size, at, s in zip(names, sizes, source, steps):
            to = at + s
            if name == "gz" and not 0 <= to < size:
                inside = False
            target = target * size + to % size
        if inside:
            pairs.append((flat, target))
    return lax.ppermute(block, names if len(names) > 1 else names[0], pairs)


def body(fraction, velocity, charge, bead_type, well_depth, tile_list, leaving):
    frac = fraction.reshape(3, 512, 128)
    charges = charge.reshape(512, 128)
    kinds = bead_type.reshape(512, 128)
    slots = leaving.reshape(6 * MIG)
    pairs = tile_list.reshape(TILES, 2).T.reshape(2, 8, 128)
    table = jnp.pad((0.5 * LJ_A) * (well_depth + well_depth.T), ((1, 109), (1, 109)))
    lists, same, *faces = pack(pairs, frac, charges, kinds)
    ghosts = [across(face, tuple(-s for s in step)) for face, (_, step) in zip(faces, GHOSTS)]
    keep = kept(slots)
    force, *returned = forces(lists.reshape(7168), frac, charges, kinds, *ghosts, same, table, keep)
    back = [across(face, step) for face, (_, step) in zip(returned, GHOSTS)]
    pos, vel, *sent = advance(slots, force, *back, keep, frac, velocity.reshape(3, 512, 128))
    steps = ((-1, 0, 0), (1, 0, 0), (0, -1, 0), (0, 1, 0), (0, 0, -1), (0, 0, 1))
    arrivals = [across(face, step) for face, step in zip(sent, steps)]
    shape = (3, 1, 1, 1, HOME + ARRIVE)
    new_position = jnp.concatenate([pos.reshape(3, HOME)] + [a[:3] for a in arrivals], axis=1).reshape(shape)
    new_velocity = jnp.concatenate([vel.reshape(3, HOME)] + [a[3:] for a in arrivals], axis=1).reshape(shape)
    return (new_position, new_velocity)


def solution(mesh):
    cells = P("gx", "gy", "gz", None)
    lists = P("gx", "gy", "gz", None, None)
    vectors = P(None, "gx", "gy", "gz", None)
    return jax.shard_map(
        body,
        mesh=mesh,
        in_specs=(vectors, vectors, cells, cells, P(), lists, lists),
        out_specs=(vectors, vectors),
        check_vma=False,
    )
```

```python
import math
import jax
import jax.numpy as jnp
from jax import lax
from jax.experimental import pallas as pl
from jax.experimental.pallas import tpu as pltpu
from jax.sharding import PartitionSpec as P

CELLS = (16, 2, 16)
MIG = 128
HOME = 65536
ARRIVE = 768
STEP = 0.03
KICK = 0.03 / 144.0
BOX = (64.0, 4.0, 32.0)
C = 872
TILES = 1024
SPAN = (4.0, 2.0, 2.0)
CUTOFF2 = 1.21
NEAR2 = 1.2105
SIGMA2 = 0.2209
FLOOR2 = 0.1764
EDGE_C = (SIGMA2 / CUTOFF2) ** 3
LJ_EDGE = 24.0 * EDGE_C * (2.0 * EDGE_C - 1.0) / CUTOFF2
LJ_A = 48.0 * SIGMA2**6
LJ_B = 24.0 * SIGMA2**3
COULOMB = 138.935458 / 2.5
INV_CUT3 = 1.0 / 1.331
UNROLL = 28
ROWS = 16
LIST = 1280
ITEMS = TILES * 128 // ROWS + 16 * UNROLL
f32 = jnp.float32
bf16 = jnp.bfloat16


def split3(x):
    hi = x.astype(bf16)
    rest = x - hi.astype(f32)
    mid = rest.astype(bf16)
    low = (rest - mid.astype(f32)).astype(bf16)
    return hi, mid, low


def fold8(x):
    return sum((x[8 * m:8 * m + 8] for m in range(1, ROWS // 8)), x[0:8])


def dot_nt(a, b):
    return lax.dot_general(a, b, (((1,), (1,)), ((), ())), preferred_element_type=f32)


def force_kernel(lists, frac, charge, kind, gx, gy, gxy, gz, gyz, gxz, gxyz, same, table, keep,
                 home_out, rx, ry, rxy, rz, ryz, rxz, rxyz, corner, fields, near, dist, rank, half, offs, cnt, ax0, ax1, ax2, bx0, bx1, bx2, counts, at_tile, at_row, spread, picked, depth, eps, pulls, compact, compact2, sem):
    zero = jnp.zeros((8, 128), f32)
    acc_a, acc_b = (ax0, ax1, ax2), (bx0, bx1, bx2)

    sub8 = lax.broadcasted_iota(jnp.int32, (8, 128), 0)
    corner[...] = jnp.zeros((5, 8, 128), f32)
    corner[:, 0:2, :] = gxz[...]
    corner[:, 2:3, :] = gxyz[...]

    def load(values, first, k, cells):
        to = pl.multiple_of(first + 8 * k, 8)
        for m in range(8):
            fields[pl.ds(pl.multiple_of(8 * to + 8 * m, 8), 8), :] = zero
        for acc in acc_a + acc_b:
            for m in range(8):
                acc[pl.ds(pl.multiple_of(8 * to + 8 * m, 8), 8), :] = zero
        for f, r in enumerate(values):
            put = r + cells[f].astype(f32) * SPAN[f] if f < 3 else r
            fields[pl.ds(8 * to + f, 8, stride=8), :] = put
            if f < 3:
                s = SPAN[f] - r
                near[pl.ds(pl.multiple_of(3 * f * C + to, 8), 8), :] = r * r
                near[pl.ds(pl.multiple_of((3 * f + 1) * C + to, 8), 8), :] = zero
                near[pl.ds(pl.multiple_of((3 * f + 2) * C + to, 8), 8), :] = s * s

    def load_home(k, _):
        rows = pl.ds(pl.multiple_of(8 * k, 8), 8)
        c = 8 * k + sub8
        load(bead_values(frac, charge, kind, rows), 0, k, (c >> 5, (c >> 4) & 1, c & 15))
        return 0
    lax.fori_loop(0, 64, load_home, 0, unroll=2)
    high = jnp.full((8, 128), 16, jnp.int32)
    two = jnp.full((8, 128), 2, jnp.int32)
    for src, first, count, cells in (
        (gx, 512, 32, lambda c: (high, c >> 4, c & 15)),
        (gy, 544, 256, lambda c: (c >> 4, two, c & 15)),
        (gxy, 800, 16, lambda c: (high, two, c)),
        (gz, 816, 32, lambda c: (c >> 1, c & 1, high)),
        (gyz, 848, 16, lambda c: (c, two, high)),
        (corner, 864, 8, lambda c: (high, c, high)),
    ):
        def load_ghost(k, _, src=src, first=first, cells=cells):
            rows = pl.ds(pl.multiple_of(8 * k, 8), 8)
            load([src[f, rows, :] for f in range(5)], first, k, cells(8 * k + sub8))
            return 0
        lax.fori_loop(0, count // 8, load_ghost, 0)

    n_live = lists[5 * LIST]

    def stage(k, _):
        for m in range(32):
            t = 32 * k + m
            s = (near[pl.ds(lists[2 * LIST + t], 1), :] + near[pl.ds(lists[3 * LIST + t], 1), :]
                 + near[pl.ds(lists[4 * LIST + t], 1), :])
            dist[pl.ds(t, 1), :] = s
        return 0
    lax.fori_loop(0, (n_live + 31) // 32, stage, 0)

    below = (lax.broadcasted_iota(jnp.int32, (128, 128), 0)
             < lax.broadcasted_iota(jnp.int32, (128, 128), 1)).astype(f32).astype(bf16)
    row_id = lax.broadcasted_iota(jnp.int32, (128, 128), 0)
    ones = jnp.ones((16, 128), bf16)
    diagonal = row_id == lax.broadcasted_iota(jnp.int32, (128, 128), 1)
    for g in range(TILES // 128):
        keep = (dist[128 * g:128 * g + 128, :] < NEAR2) & (row_id + 128 * g < n_live)
        hot = jnp.where(keep, 1.0, 0.0).astype(bf16)
        before = jnp.dot(hot, below, preferred_element_type=f32)
        rank[128 * g:128 * g + 128, :] = jnp.where(keep, before, -1.0)
        cnt[g:g + 1, :] = dot_nt(ones, hot)[0:1].astype(jnp.int32)
        column = jnp.sum(jnp.where(diagonal, same[g:g + 1, :], 0.0), axis=1, keepdims=True)
        half[128 * g:128 * g + 128, :] = jnp.broadcast_to(column, (128, 128))
    rank[TILES:LIST, :] = jnp.full((LIST - TILES, 128), -1.0, f32)
    half[TILES:LIST, :] = jnp.zeros((LIST - TILES, 128), f32)
    cnt[TILES // 128:, :] = jnp.zeros((8, 128), jnp.int32)
    for g in range(LIST // 128):
        pltpu.make_async_copy(cnt.at[g], counts.at[pl.ds(128 * g, 128)], sem.at[g]).start()
    offs[...] = lax.broadcasted_iota(jnp.int32, (128, 128), 0).astype(f32)
    for g in range(LIST // 128):
        pltpu.make_async_copy(cnt.at[g], counts.at[pl.ds(128 * g, 128)], sem.at[g]).wait()

    kinds = lax.broadcasted_iota(jnp.int32, (24, 128), 0).astype(f32)
    U = UNROLL

    wr = lax.broadcasted_iota(jnp.int32, (24, 128), 0)
    spread[...] = jnp.zeros((48, 768), f32)
    for f in range(4):
        spread[0:24, 128 * f:128 * f + 128] = jnp.where((wr & 7) == f, 1.0, 0.0)
    t_hi, t_mid, _ = split3(table[0:24, :])
    spread[24:48, 512:640] = t_hi.astype(f32)
    spread[24:48, 640:768] = t_mid.astype(f32)
    weights = spread[...].astype(bf16)

    def decode(n, t, off):
        for u in range(U):
            at_tile[n * U + u] = t
            at_row[n * U + u] = off
            last = off + ROWS >= counts[t]
            t = jnp.where(last, t + 1, t)
            off = jnp.where(last, 0, off + ROWS)
        return t, off

    def chosen(t, off):
        return rank[pl.ds(t, ROWS, stride=0), :] == offs[pl.ds(pl.multiple_of(off, 8), ROWS), :]

    def select(n):
        for u in range(U):
            t, off = at_tile[n * U + u], at_row[n * U + u]
            i = lists[t]
            hot = jnp.where(chosen(t, off), 1.0, 0.0).astype(bf16)
            d = fields[pl.ds(pl.multiple_of(i, 8), 8), :]
            hi = d.astype(bf16).astype(f32)
            mid = (d - hi).astype(bf16).astype(f32)
            kind = jnp.where(fields[pl.ds(i + 4, 24, stride=0), :] == kinds, 1.0, 0.0)
            rows = jnp.concatenate([hi, mid, d - hi - mid, kind], axis=0)
            compact[ROWS * u:ROWS * u + ROWS, :] = dot_nt(hot, rows.astype(bf16)).astype(bf16)

    def well(n):
        c = compact[...]
        d = jnp.dot(c, weights[:, 512:], preferred_element_type=f32)
        depth[...] = d[:, :128] + d[:, 128:]
        compact2[...] = c

    def widen(n):
        picked[...] = jnp.dot(compact2[...], weights[:, :512], preferred_element_type=f32)

    def gather(n):
        for u in range(U):
            j = lists[LIST + at_tile[n * U + u]]
            kb = fields[pl.ds(j + 4, 8, stride=0), :].astype(jnp.int32)
            at = slice(ROWS * u, ROWS * u + ROWS)
            eps[at, :] = jnp.take_along_axis(depth[at, :], jnp.concatenate([kb] * (ROWS // 8), axis=0), axis=1)

    def interact(n):
        for u in range(U):
            t = at_tile[n * U + u]
            j = lists[LIST + t]
            at = slice(ROWS * u, ROWS * u + ROWS)
            ds = [picked[at, 128 * ax:128 * ax + 128] - fields[pl.ds(j + ax, ROWS, stride=0), :] for ax in range(3)]
            qb = fields[pl.ds(j + 3, ROWS, stride=0), :]
            dx, dy, dz = ds
            r2 = dx * dx + dy * dy + dz * dz
            s2 = jnp.maximum(r2, FLOOR2)
            y = lax.rsqrt(s2)
            v = y * y
            v3 = v * v * v
            lj = (v3 - LJ_B / LJ_A) * (v3 * v) - LJ_EDGE / LJ_A
            g = eps[at, :] * lj + (picked[at, 384:512] * qb) * (v * y - INV_CUT3)
            g = jnp.where(r2 < CUTOFF2, g * half[pl.ds(t, ROWS, stride=0), :], 0.0)
            b_rows = pl.ds(pl.multiple_of(j, 8), 8)
            for f in range(3):
                ws = g * ds[f]
                pulls[at, 128 * f:128 * f + 128] = ws
                acc_b[f][b_rows, :] = acc_b[f][b_rows, :] + fold8(ws)

    def gain(n):
        for u in range(U):
            t, off = at_tile[n * U + u], at_row[n * U + u]
            at = slice(ROWS * u, ROWS * u + ROWS)
            sel = chosen(t, off)
            a_rows = pl.ds(pl.multiple_of(lists[t], 8), 8)
            for f in range(3):
                row = jnp.sum(pulls[at, 128 * f:128 * f + 128], axis=1, keepdims=True)
                acc_a[f][a_rows, :] = acc_a[f][a_rows, :] + fold8(jnp.where(sel, row, 0.0))

    for ref in (picked, depth, eps, pulls, compact, compact2):
        ref[...] = jnp.zeros(ref.shape, ref.dtype)
    for u in range(5 * U):
        at_tile[u] = TILES
        at_row[u] = 0

    def work(state):
        n, t, off = state
        t, off = decode(n + 5, t, off)
        gain(n)
        interact(n + 1)
        gather(n + 2)
        widen(n + 2)
        well(n + 3)
        select(n + 4)
        return n + 1, t, off

    lax.while_loop(lambda s: (s[0] < 5) | (at_tile[s[0] * U] < n_live), work, (n_live * 0, n_live * 0, n_live * 0))

    def folded(f, row):
        a = acc_a[f][pl.ds(8 * row, 8, stride=8), :]
        b = acc_b[f][pl.ds(8 * row, 8, stride=8), :]
        for m in range(1, 8):
            a = a + acc_a[f][pl.ds(8 * row + m, 8, stride=8), :]
            b = b + acc_b[f][pl.ds(8 * row + m, 8, stride=8), :]
        return a - b

    for f in range(3):
        for to, first, count in (
            (home_out, 0, 512), (rx, 512, 32), (ry, 544, 256), (rxy, 800, 16), (rz, 816, 32), (ryz, 848, 16),
        ):
            def give(k, _, f=f, to=to, first=first):
                to[f, pl.ds(pl.multiple_of(8 * k, 8), 8), :] = folded(f, first + 8 * k)
                return 0
            lax.fori_loop(0, count // 8, give, 0, unroll=min(4, count // 8))
        last = folded(f, 864)
        rxz[f] = last[0:2]
        rxyz[f] = last[2:3]


def bead_values(frac, charge, kind, rows):
    values = [frac[f, rows, :] * SPAN[f] for f in range(3)]
    return values + [charge[rows, :] * math.sqrt(COULOMB), (kind[rows, :] + 1).astype(f32)]


GHOSTS = ((32, (1, 0, 0)), (256, (0, 1, 0)), (16, (1, 1, 0)), (32, (0, 0, 1)), (16, (0, 1, 1)), (2, (1, 0, 1)), (1, (1, 1, 1)))


def forces(lists, *arrays):
    vm = pl.BlockSpec(memory_space=pltpu.VMEM)
    sm = pl.BlockSpec(memory_space=pltpu.SMEM)
    return pl.pallas_call(
        force_kernel,
        out_shape=[jax.ShapeDtypeStruct((3, n, 128), f32) for n in (512,) + tuple(n for n, _ in GHOSTS)],
        in_specs=[sm] + [vm] * (len(arrays) - 1) + [pl.BlockSpec(memory_space=pl.ANY)],
        out_specs=[vm] * 8,
        scratch_shapes=[
            pltpu.VMEM((5, 8, 128), f32),
            pltpu.VMEM((8 * C, 128), f32),
            pltpu.VMEM((9 * C, 128), f32),
            pltpu.VMEM((TILES, 128), f32),
            pltpu.VMEM((LIST, 128), f32),
            pltpu.VMEM((LIST, 128), f32),
            pltpu.VMEM((128, 128), f32),
            pltpu.VMEM((16, 128), jnp.int32),
            *[pltpu.VMEM((8 * C, 128), f32)] * 6,
            pltpu.SMEM((LIST,), jnp.int32),
            pltpu.SMEM((ITEMS,), jnp.int32),
            pltpu.SMEM((ITEMS,), jnp.int32),
            pltpu.VMEM((48, 768), f32),
            pltpu.VMEM((ROWS * UNROLL, 512), f32),
            pltpu.VMEM((ROWS * UNROLL, 128), f32),
            pltpu.VMEM((ROWS * UNROLL, 128), f32),
            pltpu.VMEM((ROWS * UNROLL, 384), f32),
            pltpu.VMEM((ROWS * UNROLL, 48), bf16),
            pltpu.VMEM((ROWS * UNROLL, 48), bf16),
            pltpu.SemaphoreType.DMA((LIST // 128,)),
        ],
        compiler_params=pltpu.CompilerParams(vmem_limit_bytes=56 * 2**20),
        name="pair_forces",
    )(lists, *arrays)


def pack_kernel(pairs, frac, charge, kind, lists, same, sx, sy, sxy, sz, syz, sxz, sxyz, beads):
    def fill(k, _):
        rows = pl.ds(pl.multiple_of(8 * k, 8), 8)
        for f, value in enumerate(bead_values(frac, charge, kind, rows)):
            beads[f, rows, :] = value
        return 0
    lax.fori_loop(0, 64, fill, 0, unroll=4)
    for f in range(5):
        sx[f] = beads[f, 0:32, :]
        for k in range(16):
            sy[f, 16 * k:16 * k + 16, :] = beads[f, 32 * k:32 * k + 16, :]
            syz[f, k:k + 1, :] = beads[f, 32 * k:32 * k + 1, :]
        sxy[f] = beads[f, 0:16, :]
        for k in range(32):
            sz[f, k:k + 1, :] = beads[f, 16 * k:16 * k + 1, :]
        sxz[f, 0:1, :] = beads[f, 0:1, :]
        sxz[f, 1:2, :] = beads[f, 16:17, :]
        sxyz[f] = beads[f, 0:1, :]

    first, second = pairs[0], pairs[1]
    lists[...] = jnp.zeros((56, 128), jnp.int32)
    count = jnp.sum((first >= 0).astype(f32), axis=(0, 1), keepdims=True)
    lists[50:51, :] = jnp.broadcast_to(count, (1, 128)).astype(jnp.int32)
    i, a = placed(jnp.maximum(first, 0))
    j, b = placed(jnp.maximum(second, 0))
    lists[0:8, :] = 8 * i
    lists[10:18, :] = 8 * j
    for f in range(3):
        lists[20 + 10 * f:28 + 10 * f, :] = (3 * f + b[f] - a[f] + 1) * C + i
    same[...] = jnp.where(first == second, 0.5, 1.0)


def placed(index):
    home, on_x, on_y = index < 512, index < 544, index < 816
    y, z = index - 544, index - 816
    zx = (z * 171) >> 9
    zy = z - 3 * zx
    bx = jnp.where(home, index >> 5, jnp.where(on_x, 16, jnp.where(on_y, y >> 4, zx)))
    by = jnp.where(home, (index >> 4) & 1, jnp.where(on_x, ((index - 512) >> 4) & 1, jnp.where(on_y, 2, zy)))
    bz = jnp.where(on_y, index & 15, 16)
    lower = jnp.where(zx < 16, 816 + 2 * zx + zy, 864 + zy)
    upper = jnp.where(zx < 16, 848 + zx, 866)
    row = jnp.where(on_y, index, jnp.where(zy < 2, lower, upper))
    return row, (bx, by, bz)


def pack(*arrays):
    vm = pl.BlockSpec(memory_space=pltpu.VMEM)
    return pl.pallas_call(
        pack_kernel,
        out_shape=[jax.ShapeDtypeStruct((56, 128), jnp.int32), jax.ShapeDtypeStruct((8, 128), f32)]
        + [jax.ShapeDtypeStruct((5, n, 128), f32) for n, _ in GHOSTS],
        in_specs=[vm] * len(arrays),
        out_specs=[vm] * 9,
        scratch_shapes=[pltpu.VMEM((5, 512, 128), f32)],
        compiler_params=pltpu.CompilerParams(vmem_limit_bytes=40 * 2**20),
        name="pack",
    )(*arrays)


def keep_kernel(leaving, keep, *marks):
    lane = lax.broadcasted_iota(jnp.int32, (1, 128), 1)
    for mark in marks:
        mark[...] = jnp.ones((512, 128), f32)

    def drop(k, _):
        for u in range(4):
            for face, mark in enumerate(marks):
                slot = leaving[face * MIG + 4 * k + u]
                at = jnp.maximum(slot, 0)
                row = pl.ds(at >> 7, 1)
                mark[row, :] = jnp.where(lane == jnp.where(slot >= 0, at & 127, -1), 0.0, mark[row, :])
        return 0
    lax.fori_loop(0, MIG // 4, drop, 0)
    product = marks[0][...]
    for mark in marks[1:]:
        product = product * mark[...]
    keep[...] = product


def kept(leaving):
    return pl.pallas_call(
        keep_kernel,
        out_shape=jax.ShapeDtypeStruct((512, 128), f32),
        in_specs=[pl.BlockSpec(memory_space=pltpu.SMEM)],
        out_specs=pl.BlockSpec(memory_space=pltpu.VMEM),
        scratch_shapes=[pltpu.VMEM((512, 128), f32)] * 6,
        cost_estimate=pl.CostEstimate(flops=10**6, bytes_accessed=262144, transcendentals=0),
        name="kept",
    )(leaving)


def advance_kernel(leaving, force, bx, by, bxy, bz, byz, bxz, bxyz, keep, fraction, velocity,
                   pos, vel, s0, s1, s2, s3, s4, s5, total, beads):
    for f in range(3):
        total[f] = force[f]
        total[f, 0:32, :] = total[f, 0:32, :] + bx[f]
        for k in range(16):
            total[f, 32 * k:32 * k + 16, :] = total[f, 32 * k:32 * k + 16, :] + by[f, 16 * k:16 * k + 16, :]
        total[f, 0:16, :] = total[f, 0:16, :] + bxy[f]
        for k in range(32):
            total[f, 16 * k:16 * k + 1, :] = total[f, 16 * k:16 * k + 1, :] + bz[f, k:k + 1, :]
        for k in range(16):
            total[f, 32 * k:32 * k + 1, :] = total[f, 32 * k:32 * k + 1, :] + byz[f, k:k + 1, :]
        for k in range(2):
            total[f, 16 * k:16 * k + 1, :] = total[f, 16 * k:16 * k + 1, :] + bxz[f, k:k + 1, :]
        total[f, 0:1, :] = total[f, 0:1, :] + bxyz[f]

    sub = lax.broadcasted_iota(jnp.int32, (8, 128), 0)
    lane = lax.broadcasted_iota(jnp.int32, (8, 128), 1)

    def move(k, _):
        rows = pl.ds(pl.multiple_of(8 * k, 8), 8)
        cluster = 8 * k + sub
        cells = (cluster >> 5, (cluster >> 4) & 1, cluster & 15)
        for f in range(3):
            half = velocity[f, rows, :] + KICK * total[f, rows, :]
            place = (cells[f].astype(f32) + fraction[f, rows, :]) * SPAN[f] + STEP * half
            beads[pl.ds(64 * k + f, 8, stride=8), :] = place
            beads[pl.ds(64 * k + 3 + f, 8, stride=8), :] = half
            pos[f, rows, :] = place * keep[rows, :]
            vel[f, rows, :] = half * keep[rows, :]
        return 0
    lax.fori_loop(0, 64, move, 0, unroll=2)

    for face, sent in enumerate((s0, s1, s2, s3, s4, s5)):
        span = BOX[face // 2] if face % 2 == 0 else -BOX[face // 2]
        shift = jnp.where(sub == face // 2, span, 0.0)

        def pick(k, taken, face=face, shift=shift):
            for u in range(8):
                m = 8 * k + u
                slot = leaving[face * MIG + m]
                at = jnp.maximum(slot, 0)
                row = beads[pl.ds(pl.multiple_of((at >> 7) * 8, 8), 8), :]
                row = pltpu.roll(row, (m - at) & 127, 1) + shift
                taken = jnp.where(lane == jnp.where(slot >= 0, m, -1), row, taken)
            return taken
        taken = lax.fori_loop(0, MIG // 8, pick, jnp.zeros((8, 128), f32), unroll=4)
        sent[...] = taken[0:6]


def advance(leaving, *arrays):
    vm = pl.BlockSpec(memory_space=pltpu.VMEM)
    sm = pl.BlockSpec(memory_space=pltpu.SMEM)
    return pl.pallas_call(
        advance_kernel,
        out_shape=[jax.ShapeDtypeStruct((3, 512, 128), f32)] * 2 + [jax.ShapeDtypeStruct((6, 128), f32)] * 6,
        in_specs=[sm] + [vm] * len(arrays),
        out_specs=[vm] * 8,
        scratch_shapes=[pltpu.VMEM((3, 512, 128), f32), pltpu.VMEM((4096, 128), f32)],
        compiler_params=pltpu.CompilerParams(vmem_limit_bytes=40 * 2**20),
        name="advance",
    )(leaving, *arrays)


def across(block, step):
    names = tuple(n for n, s in zip(("gx", "gy", "gz"), step) if s)
    steps = [s for s in step if s]
    sizes = [lax.axis_size(n) for n in names]
    pairs = []
    for flat in range(math.prod(sizes)):
        rest, source = flat, []
        for size in reversed(sizes):
            source.insert(0, rest % size)
            rest //= size
        target = 0
        inside = True
        for name, size, at, s in zip(names, sizes, source, steps):
            to = at + s
            if name == "gz" and not 0 <= to < size:
                inside = False
            target = target * size + to % size
        if inside:
            pairs.append((flat, target))
    return lax.ppermute(block, names if len(names) > 1 else names[0], pairs)


def body(fraction, velocity, charge, bead_type, well_depth, tile_list, leaving):
    frac = fraction.reshape(3, 512, 128)
    charges = charge.reshape(512, 128)
    kinds = bead_type.reshape(512, 128)
    slots = leaving.reshape(6 * MIG)
    pairs = tile_list.reshape(TILES, 2).T.reshape(2, 8, 128)
    table = jnp.pad((0.5 * LJ_A) * (well_depth + well_depth.T), ((1, 109), (1, 109)))
    lists, same, *faces = pack(pairs, frac, charges, kinds)
    ghosts = [across(face, tuple(-s for s in step)) for face, (_, step) in zip(faces, GHOSTS)]
    keep = kept(slots)
    force, *returned = forces(lists.reshape(7168), frac, charges, kinds, *ghosts, same, table, keep)
    back = [across(face, step) for face, (_, step) in zip(returned, GHOSTS)]
    pos, vel, *sent = advance(slots, force, *back, keep, frac, velocity.reshape(3, 512, 128))
    steps = ((-1, 0, 0), (1, 0, 0), (0, -1, 0), (0, 1, 0), (0, 0, -1), (0, 0, 1))
    arrivals = [across(face, step) for face, step in zip(sent, steps)]
    shape = (3, 1, 1, 1, HOME + ARRIVE)
    new_position = jnp.concatenate([pos.reshape(3, HOME)] + [a[:3] for a in arrivals], axis=1).reshape(shape)
    new_velocity = jnp.concatenate([vel.reshape(3, HOME)] + [a[3:] for a in arrivals], axis=1).reshape(shape)
    return (new_position, new_velocity)


def solution(mesh):
    cells = P("gx", "gy", "gz", None)
    lists = P("gx", "gy", "gz", None, None)
    vectors = P(None, "gx", "gy", "gz", None)
    return jax.shard_map(
        body,
        mesh=mesh,
        in_specs=(vectors, vectors, cells, cells, P(), lists, lists),
        out_specs=(vectors, vectors),
        check_vma=False,
    )
```

```python
import math
import jax
import jax.numpy as jnp
from jax import lax
from jax.experimental import pallas as pl
from jax.experimental.pallas import tpu as pltpu
from jax.sharding import PartitionSpec as P

CELLS = (16, 2, 16)
MIG = 128
HOME = 65536
ARRIVE = 768
STEP = 0.03
KICK = 0.03 / 144.0
BOX = (64.0, 4.0, 32.0)
C = 872
TILES = 1024
SPAN = (4.0, 2.0, 2.0)
CUTOFF2 = 1.21
NEAR2 = 1.2105
SIGMA2 = 0.2209
FLOOR2 = 0.1764
EDGE_C = (SIGMA2 / CUTOFF2) ** 3
LJ_EDGE = 24.0 * EDGE_C * (2.0 * EDGE_C - 1.0) / CUTOFF2
LJ_A = 48.0 * SIGMA2**6
LJ_B = 24.0 * SIGMA2**3
COULOMB = 138.935458 / 2.5
INV_CUT3 = 1.0 / 1.331
UNROLL = 28
ROWS = 16
LIST = 1280
ITEMS = TILES * 128 // ROWS + 16 * UNROLL
f32 = jnp.float32
bf16 = jnp.bfloat16


def split3(x):
    hi = x.astype(bf16)
    rest = x - hi.astype(f32)
    mid = rest.astype(bf16)
    low = (rest - mid.astype(f32)).astype(bf16)
    return hi, mid, low


def fold8(x):
    return sum((x[8 * m:8 * m + 8] for m in range(1, ROWS // 8)), x[0:8])


def dot_nt(a, b):
    return lax.dot_general(a, b, (((1,), (1,)), ((), ())), preferred_element_type=f32)


def force_kernel(lists, frac, charge, kind, gx, gy, gxy, gz, gyz, gxz, gxyz, same, table, keep,
                 home_out, rx, ry, rxy, rz, ryz, rxz, rxyz, corner, fields, near, dist, rank, half, offs, cnt, ax0, ax1, ax2, bx0, bx1, bx2, counts, at_tile, at_row, spread, picked, depth, eps, pulls, compact, compact2, sem):
    zero = jnp.zeros((8, 128), f32)
    acc_a, acc_b = (ax0, ax1, ax2), (bx0, bx1, bx2)

    sub8 = lax.broadcasted_iota(jnp.int32, (8, 128), 0)
    corner[...] = jnp.zeros((5, 8, 128), f32)
    corner[:, 0:2, :] = gxz[...]
    corner[:, 2:3, :] = gxyz[...]

    def load(values, first, k, cells):
        to = pl.multiple_of(first + 8 * k, 8)
        for m in range(8):
            fields[pl.ds(pl.multiple_of(8 * to + 8 * m, 8), 8), :] = zero
        for acc in acc_a + acc_b:
            for m in range(8):
                acc[pl.ds(pl.multiple_of(8 * to + 8 * m, 8), 8), :] = zero
        for f, r in enumerate(values):
            put = r + cells[f].astype(f32) * SPAN[f] if f < 3 else r
            fields[pl.ds(8 * to + f, 8, stride=8), :] = put
            if f < 3:
                s = SPAN[f] - r
                near[pl.ds(pl.multiple_of(3 * f * C + to, 8), 8), :] = r * r
                near[pl.ds(pl.multiple_of((3 * f + 1) * C + to, 8), 8), :] = zero
                near[pl.ds(pl.multiple_of((3 * f + 2) * C + to, 8), 8), :] = s * s

    def load_home(k, _):
        rows = pl.ds(pl.multiple_of(8 * k, 8), 8)
        c = 8 * k + sub8
        load(bead_values(frac, charge, kind, rows), 0, k, (c >> 5, (c >> 4) & 1, c & 15))
        return 0
    lax.fori_loop(0, 64, load_home, 0, unroll=2)
    high = jnp.full((8, 128), 16, jnp.int32)
    two = jnp.full((8, 128), 2, jnp.int32)
    for src, first, count, cells in (
        (gx, 512, 32, lambda c: (high, c >> 4, c & 15)),
        (gy, 544, 256, lambda c: (c >> 4, two, c & 15)),
        (gxy, 800, 16, lambda c: (high, two, c)),
        (gz, 816, 32, lambda c: (c >> 1, c & 1, high)),
        (gyz, 848, 16, lambda c: (c, two, high)),
        (corner, 864, 8, lambda c: (high, c, high)),
    ):
        def load_ghost(k, _, src=src, first=first, cells=cells):
            rows = pl.ds(pl.multiple_of(8 * k, 8), 8)
            load([src[f, rows, :] for f in range(5)], first, k, cells(8 * k + sub8))
            return 0
        lax.fori_loop(0, count // 8, load_ghost, 0)

    n_live = lists[5 * LIST]

    def stage(k, _):
        for m in range(32):
            t = 32 * k + m
            s = (near[pl.ds(lists[2 * LIST + t], 1), :] + near[pl.ds(lists[3 * LIST + t], 1), :]
                 + near[pl.ds(lists[4 * LIST + t], 1), :])
            dist[pl.ds(t, 1), :] = s
        return 0
    lax.fori_loop(0, (n_live + 31) // 32, stage, 0)

    below = (lax.broadcasted_iota(jnp.int32, (128, 128), 0)
             < lax.broadcasted_iota(jnp.int32, (128, 128), 1)).astype(f32).astype(bf16)
    row_id = lax.broadcasted_iota(jnp.int32, (128, 128), 0)
    ones = jnp.ones((16, 128), bf16)
    diagonal = row_id == lax.broadcasted_iota(jnp.int32, (128, 128), 1)
    for g in range(TILES // 128):
        keep = (dist[128 * g:128 * g + 128, :] < NEAR2) & (row_id + 128 * g < n_live)
        hot = jnp.where(keep, 1.0, 0.0).astype(bf16)
        before = jnp.dot(hot, below, preferred_element_type=f32)
        rank[128 * g:128 * g + 128, :] = jnp.where(keep, before, -1.0)
        cnt[g:g + 1, :] = dot_nt(ones, hot)[0:1].astype(jnp.int32)
        column = jnp.sum(jnp.where(diagonal, same[g:g + 1, :], 0.0), axis=1, keepdims=True)
        half[128 * g:128 * g + 128, :] = jnp.broadcast_to(column, (128, 128))
    rank[TILES:LIST, :] = jnp.full((LIST - TILES, 128), -1.0, f32)
    half[TILES:LIST, :] = jnp.zeros((LIST - TILES, 128), f32)
    cnt[TILES // 128:, :] = jnp.zeros((8, 128), jnp.int32)
    for g in range(LIST // 128):
        pltpu.make_async_copy(cnt.at[g], counts.at[pl.ds(128 * g, 128)], sem.at[g]).start()
    offs[...] = lax.broadcasted_iota(jnp.int32, (128, 128), 0).astype(f32)
    for g in range(LIST // 128):
        pltpu.make_async_copy(cnt.at[g], counts.at[pl.ds(128 * g, 128)], sem.at[g]).wait()

    kinds = lax.broadcasted_iota(jnp.int32, (24, 128), 0).astype(f32)
    U = UNROLL

    wr = lax.broadcasted_iota(jnp.int32, (24, 128), 0)
    spread[...] = jnp.zeros((48, 768), f32)
    for f in range(4):
        spread[0:24, 128 * f:128 * f + 128] = jnp.where((wr & 7) == f, 1.0, 0.0)
    t_hi, t_mid, _ = split3(table[0:24, :])
    spread[24:48, 512:640] = t_hi.astype(f32)
    spread[24:48, 640:768] = t_mid.astype(f32)
    weights = spread[...].astype(bf16)

    def decode(n, t, off):
        for u in range(U):
            at_tile[n * U + u] = t
            at_row[n * U + u] = off
            last = off + ROWS >= counts[t]
            t = jnp.where(last, t + 1, t)
            off = jnp.where(last, 0, off + ROWS)
        return t, off

    def chosen(t, off):
        return rank[pl.ds(t, ROWS, stride=0), :] == offs[pl.ds(pl.multiple_of(off, 8), ROWS), :]

    def select(n):
        for u in range(U):
            t, off = at_tile[n * U + u], at_row[n * U + u]
            i = lists[t]
            hot = jnp.where(chosen(t, off), 1.0, 0.0).astype(bf16)
            d = fields[pl.ds(pl.multiple_of(i, 8), 8), :]
            hi = d.astype(bf16).astype(f32)
            mid = (d - hi).astype(bf16).astype(f32)
            kind = jnp.where(fields[pl.ds(i + 4, 24, stride=0), :] == kinds, 1.0, 0.0)
            rows = jnp.concatenate([hi, mid, d - hi - mid, kind], axis=0)
            compact[ROWS * u:ROWS * u + ROWS, :] = dot_nt(hot, rows.astype(bf16)).astype(bf16)

    def well(n):
        c = compact[...]
        d = jnp.dot(c, weights[:, 512:], preferred_element_type=f32)
        depth[...] = d[:, :128] + d[:, 128:]
        compact2[...] = c

    def widen(n):
        picked[...] = jnp.dot(compact2[...], weights[:, :512], preferred_element_type=f32)

    def gather(n):
        for u in range(U):
            j = lists[LIST + at_tile[n * U + u]]
            kb = fields[pl.ds(j + 4, 8, stride=0), :].astype(jnp.int32)
            at = slice(ROWS * u, ROWS * u + ROWS)
            eps[at, :] = jnp.take_along_axis(depth[at, :], jnp.concatenate([kb] * (ROWS // 8), axis=0), axis=1)

    def interact(n):
        for u in range(U):
            t = at_tile[n * U + u]
            j = lists[LIST + t]
            at = slice(ROWS * u, ROWS * u + ROWS)
            ds = [picked[at, 128 * ax:128 * ax + 128] - fields[pl.ds(j + ax, ROWS, stride=0), :] for ax in range(3)]
            qb = fields[pl.ds(j + 3, ROWS, stride=0), :]
            dx, dy, dz = ds
            r2 = dx * dx + dy * dy + dz * dz
            s2 = jnp.maximum(r2, FLOOR2)
            y = lax.rsqrt(s2)
            v = y * y
            v3 = v * v * v
            lj = (v3 - LJ_B / LJ_A) * (v3 * v) - LJ_EDGE / LJ_A
            g = eps[at, :] * lj + (picked[at, 384:512] * qb) * (v * y - INV_CUT3)
            g = jnp.where(r2 < CUTOFF2, g * half[pl.ds(t, ROWS, stride=0), :], 0.0)
            b_rows = pl.ds(pl.multiple_of(j, 8), 8)
            for f in range(3):
                ws = g * ds[f]
                pulls[at, 128 * f:128 * f + 128] = ws
                acc_b[f][b_rows, :] = acc_b[f][b_rows, :] + fold8(ws)

    def gain(n):
        for u in range(U):
            t, off = at_tile[n * U + u], at_row[n * U + u]
            at = slice(ROWS * u, ROWS * u + ROWS)
            sel = chosen(t, off)
            a_rows = pl.ds(pl.multiple_of(lists[t], 8), 8)
            for f in range(3):
                row = jnp.sum(pulls[at, 128 * f:128 * f + 128], axis=1, keepdims=True)
                acc_a[f][a_rows, :] = acc_a[f][a_rows, :] + fold8(jnp.where(sel, row, 0.0))

    for ref in (picked, depth, eps, pulls, compact, compact2):
        ref[...] = jnp.zeros(ref.shape, ref.dtype)
    for u in range(5 * U):
        at_tile[u] = TILES
        at_row[u] = 0

    def work(state):
        n, t, off = state
        t, off = decode(n + 5, t, off)
        gain(n)
        interact(n + 1)
        gather(n + 2)
        widen(n + 2)
        well(n + 3)
        select(n + 4)
        return n + 1, t, off

    lax.while_loop(lambda s: (s[0] < 5) | (at_tile[s[0] * U] < n_live), work, (n_live * 0, n_live * 0, n_live * 0))

    def folded(f, row):
        a = acc_a[f][pl.ds(8 * row, 8, stride=8), :]
        b = acc_b[f][pl.ds(8 * row, 8, stride=8), :]
        for m in range(1, 8):
            a = a + acc_a[f][pl.ds(8 * row + m, 8, stride=8), :]
            b = b + acc_b[f][pl.ds(8 * row + m, 8, stride=8), :]
        return a - b

    for f in range(3):
        for to, first, count in (
            (home_out, 0, 512), (rx, 512, 32), (ry, 544, 256), (rxy, 800, 16), (rz, 816, 32), (ryz, 848, 16),
        ):
            def give(k, _, f=f, to=to, first=first):
                to[f, pl.ds(pl.multiple_of(8 * k, 8), 8), :] = folded(f, first + 8 * k)
                return 0
            lax.fori_loop(0, count // 8, give, 0, unroll=min(4, count // 8))
        last = folded(f, 864)
        rxz[f] = last[0:2]
        rxyz[f] = last[2:3]


def bead_values(frac, charge, kind, rows):
    values = [frac[f, rows, :] * SPAN[f] for f in range(3)]
    return values + [charge[rows, :] * math.sqrt(COULOMB), (kind[rows, :] + 1).astype(f32)]


GHOSTS = ((32, (1, 0, 0)), (256, (0, 1, 0)), (16, (1, 1, 0)), (32, (0, 0, 1)), (16, (0, 1, 1)), (2, (1, 0, 1)), (1, (1, 1, 1)))


def forces(lists, *arrays):
    vm = pl.BlockSpec(memory_space=pltpu.VMEM)
    sm = pl.BlockSpec(memory_space=pltpu.SMEM)
    return pl.pallas_call(
        force_kernel,
        out_shape=[jax.ShapeDtypeStruct((3, n, 128), f32) for n in (512,) + tuple(n for n, _ in GHOSTS)],
        in_specs=[sm] + [vm] * (len(arrays) - 1) + [pl.BlockSpec(memory_space=pl.ANY)],
        out_specs=[vm] * 8,
        scratch_shapes=[
            pltpu.VMEM((5, 8, 128), f32),
            pltpu.VMEM((8 * C, 128), f32),
            pltpu.VMEM((9 * C, 128), f32),
            pltpu.VMEM((TILES, 128), f32),
            pltpu.VMEM((LIST, 128), f32),
            pltpu.VMEM((LIST, 128), f32),
            pltpu.VMEM((128, 128), f32),
            pltpu.VMEM((16, 128), jnp.int32),
            *[pltpu.VMEM((8 * C, 128), f32)] * 6,
            pltpu.SMEM((LIST,), jnp.int32),
            pltpu.SMEM((ITEMS,), jnp.int32),
            pltpu.SMEM((ITEMS,), jnp.int32),
            pltpu.VMEM((48, 768), f32),
            pltpu.VMEM((ROWS * UNROLL, 512), f32),
            pltpu.VMEM((ROWS * UNROLL, 128), f32),
            pltpu.VMEM((ROWS * UNROLL, 128), f32),
            pltpu.VMEM((ROWS * UNROLL, 384), f32),
            pltpu.VMEM((ROWS * UNROLL, 48), bf16),
            pltpu.VMEM((ROWS * UNROLL, 48), bf16),
            pltpu.SemaphoreType.DMA((LIST // 128,)),
        ],
        compiler_params=pltpu.CompilerParams(vmem_limit_bytes=56 * 2**20),
        name="pair_forces",
    )(lists, *arrays)


def pack_kernel(pairs, frac, charge, kind, wells, lists, same, table, sx, sy, sxy, sz, syz, sxz, sxyz, beads, square):
    square[...] = jnp.zeros((128, 128), f32)
    square[1:19, 1:19] = wells[...]
    table[...] = (0.5 * LJ_A) * (square[...] + square[...].T)

    def fill(k, _):
        rows = pl.ds(pl.multiple_of(8 * k, 8), 8)
        for f, value in enumerate(bead_values(frac, charge, kind, rows)):
            beads[f, rows, :] = value
        return 0
    lax.fori_loop(0, 64, fill, 0, unroll=4)
    for f in range(5):
        sx[f] = beads[f, 0:32, :]
        for k in range(16):
            sy[f, 16 * k:16 * k + 16, :] = beads[f, 32 * k:32 * k + 16, :]
            syz[f, k:k + 1, :] = beads[f, 32 * k:32 * k + 1, :]
        sxy[f] = beads[f, 0:16, :]
        for k in range(32):
            sz[f, k:k + 1, :] = beads[f, 16 * k:16 * k + 1, :]
        sxz[f, 0:1, :] = beads[f, 0:1, :]
        sxz[f, 1:2, :] = beads[f, 16:17, :]
        sxyz[f] = beads[f, 0:1, :]

    first, second = pairs[0], pairs[1]
    lists[...] = jnp.zeros((56, 128), jnp.int32)
    count = jnp.sum((first >= 0).astype(f32), axis=(0, 1), keepdims=True)
    lists[50:51, :] = jnp.broadcast_to(count, (1, 128)).astype(jnp.int32)
    i, a = placed(jnp.maximum(first, 0))
    j, b = placed(jnp.maximum(second, 0))
    lists[0:8, :] = 8 * i
    lists[10:18, :] = 8 * j
    for f in range(3):
        lists[20 + 10 * f:28 + 10 * f, :] = (3 * f + b[f] - a[f] + 1) * C + i
    same[...] = jnp.where(first == second, 0.5, 1.0)


def placed(index):
    home, on_x, on_y = index < 512, index < 544, index < 816
    y, z = index - 544, index - 816
    zx = (z * 171) >> 9
    zy = z - 3 * zx
    bx = jnp.where(home, index >> 5, jnp.where(on_x, 16, jnp.where(on_y, y >> 4, zx)))
    by = jnp.where(home, (index >> 4) & 1, jnp.where(on_x, ((index - 512) >> 4) & 1, jnp.where(on_y, 2, zy)))
    bz = jnp.where(on_y, index & 15, 16)
    lower = jnp.where(zx < 16, 816 + 2 * zx + zy, 864 + zy)
    upper = jnp.where(zx < 16, 848 + zx, 866)
    row = jnp.where(on_y, index, jnp.where(zy < 2, lower, upper))
    return row, (bx, by, bz)


def pack(*arrays):
    vm = pl.BlockSpec(memory_space=pltpu.VMEM)
    return pl.pallas_call(
        pack_kernel,
        out_shape=[jax.ShapeDtypeStruct((56, 128), jnp.int32), jax.ShapeDtypeStruct((8, 128), f32), jax.ShapeDtypeStruct((128, 128), f32)]
        + [jax.ShapeDtypeStruct((5, n, 128), f32) for n, _ in GHOSTS],
        in_specs=[vm] * len(arrays),
        out_specs=[vm] * 10,
        scratch_shapes=[pltpu.VMEM((5, 512, 128), f32), pltpu.VMEM((128, 128), f32)],
        compiler_params=pltpu.CompilerParams(vmem_limit_bytes=40 * 2**20),
        name="pack",
    )(*arrays)


def keep_kernel(leaving, keep, *marks):
    lane = lax.broadcasted_iota(jnp.int32, (1, 128), 1)
    for mark in marks:
        mark[...] = jnp.ones((512, 128), f32)

    def drop(k, _):
        for u in range(4):
            for face, mark in enumerate(marks):
                slot = leaving[face * MIG + 4 * k + u]
                at = jnp.maximum(slot, 0)
                row = pl.ds(at >> 7, 1)
                mark[row, :] = jnp.where(lane == jnp.where(slot >= 0, at & 127, -1), 0.0, mark[row, :])
        return 0
    lax.fori_loop(0, MIG // 4, drop, 0)
    product = marks[0][...]
    for mark in marks[1:]:
        product = product * mark[...]
    keep[...] = product


def kept(leaving):
    return pl.pallas_call(
        keep_kernel,
        out_shape=jax.ShapeDtypeStruct((512, 128), f32),
        in_specs=[pl.BlockSpec(memory_space=pltpu.SMEM)],
        out_specs=pl.BlockSpec(memory_space=pltpu.VMEM),
        scratch_shapes=[pltpu.VMEM((512, 128), f32)] * 6,
        cost_estimate=pl.CostEstimate(flops=10**6, bytes_accessed=262144, transcendentals=0),
        name="kept",
    )(leaving)


def advance_kernel(leaving, force, bx, by, bxy, bz, byz, bxz, bxyz, keep, fraction, velocity,
                   pos, vel, s0, s1, s2, s3, s4, s5, total, beads):
    for f in range(3):
        total[f] = force[f]
        total[f, 0:32, :] = total[f, 0:32, :] + bx[f]
        for k in range(16):
            total[f, 32 * k:32 * k + 16, :] = total[f, 32 * k:32 * k + 16, :] + by[f, 16 * k:16 * k + 16, :]
        total[f, 0:16, :] = total[f, 0:16, :] + bxy[f]
        for k in range(32):
            total[f, 16 * k:16 * k + 1, :] = total[f, 16 * k:16 * k + 1, :] + bz[f, k:k + 1, :]
        for k in range(16):
            total[f, 32 * k:32 * k + 1, :] = total[f, 32 * k:32 * k + 1, :] + byz[f, k:k + 1, :]
        for k in range(2):
            total[f, 16 * k:16 * k + 1, :] = total[f, 16 * k:16 * k + 1, :] + bxz[f, k:k + 1, :]
        total[f, 0:1, :] = total[f, 0:1, :] + bxyz[f]

    sub = lax.broadcasted_iota(jnp.int32, (8, 128), 0)
    lane = lax.broadcasted_iota(jnp.int32, (8, 128), 1)

    def move(k, _):
        rows = pl.ds(pl.multiple_of(8 * k, 8), 8)
        cluster = 8 * k + sub
        cells = (cluster >> 5, (cluster >> 4) & 1, cluster & 15)
        for f in range(3):
            half = velocity[f, rows, :] + KICK * total[f, rows, :]
            place = (cells[f].astype(f32) + fraction[f, rows, :]) * SPAN[f] + STEP * half
            beads[pl.ds(64 * k + f, 8, stride=8), :] = place
            beads[pl.ds(64 * k + 3 + f, 8, stride=8), :] = half
            pos[f, rows, :] = place * keep[rows, :]
            vel[f, rows, :] = half * keep[rows, :]
        return 0
    lax.fori_loop(0, 64, move, 0, unroll=2)

    for face, sent in enumerate((s0, s1, s2, s3, s4, s5)):
        span = BOX[face // 2] if face % 2 == 0 else -BOX[face // 2]
        shift = jnp.where(sub == face // 2, span, 0.0)

        def pick(k, taken, face=face, shift=shift):
            for u in range(8):
                m = 8 * k + u
                slot = leaving[face * MIG + m]
                at = jnp.maximum(slot, 0)
                row = beads[pl.ds(pl.multiple_of((at >> 7) * 8, 8), 8), :]
                row = pltpu.roll(row, (m - at) & 127, 1) + shift
                taken = jnp.where(lane == jnp.where(slot >= 0, m, -1), row, taken)
            return taken
        taken = lax.fori_loop(0, MIG // 8, pick, jnp.zeros((8, 128), f32), unroll=4)
        sent[...] = taken[0:6]


def advance(leaving, *arrays):
    vm = pl.BlockSpec(memory_space=pltpu.VMEM)
    sm = pl.BlockSpec(memory_space=pltpu.SMEM)
    return pl.pallas_call(
        advance_kernel,
        out_shape=[jax.ShapeDtypeStruct((3, 512, 128), f32)] * 2 + [jax.ShapeDtypeStruct((6, 128), f32)] * 6,
        in_specs=[sm] + [vm] * len(arrays),
        out_specs=[vm] * 8,
        scratch_shapes=[pltpu.VMEM((3, 512, 128), f32), pltpu.VMEM((4096, 128), f32)],
        compiler_params=pltpu.CompilerParams(vmem_limit_bytes=40 * 2**20),
        name="advance",
    )(leaving, *arrays)


def across(block, step):
    names = tuple(n for n, s in zip(("gx", "gy", "gz"), step) if s)
    steps = [s for s in step if s]
    sizes = [lax.axis_size(n) for n in names]
    pairs = []
    for flat in range(math.prod(sizes)):
        rest, source = flat, []
        for size in reversed(sizes):
            source.insert(0, rest % size)
            rest //= size
        target = 0
        inside = True
        for name, size, at, s in zip(names, sizes, source, steps):
            to = at + s
            if name == "gz" and not 0 <= to < size:
                inside = False
            target = target * size + to % size
        if inside:
            pairs.append((flat, target))
    return lax.ppermute(block, names if len(names) > 1 else names[0], pairs)


def body(fraction, velocity, charge, bead_type, well_depth, tile_list, leaving):
    frac = fraction.reshape(3, 512, 128)
    charges = charge.reshape(512, 128)
    kinds = bead_type.reshape(512, 128)
    slots = leaving.reshape(6 * MIG)
    pairs = tile_list.reshape(TILES, 2).T.reshape(2, 8, 128)
    lists, same, table, *faces = pack(pairs, frac, charges, kinds, well_depth)
    ghosts = [across(face, tuple(-s for s in step)) for face, (_, step) in zip(faces, GHOSTS)]
    keep = kept(slots)
    force, *returned = forces(lists.reshape(7168), frac, charges, kinds, *ghosts, same, table, keep)
    back = [across(face, step) for face, (_, step) in zip(returned, GHOSTS)]
    pos, vel, *sent = advance(slots, force, *back, keep, frac, velocity.reshape(3, 512, 128))
    steps = ((-1, 0, 0), (1, 0, 0), (0, -1, 0), (0, 1, 0), (0, 0, -1), (0, 0, 1))
    arrivals = [across(face, step) for face, step in zip(sent, steps)]
    shape = (3, 1, 1, 1, HOME + ARRIVE)
    new_position = jnp.concatenate([pos.reshape(3, HOME)] + [a[:3] for a in arrivals], axis=1).reshape(shape)
    new_velocity = jnp.concatenate([vel.reshape(3, HOME)] + [a[3:] for a in arrivals], axis=1).reshape(shape)
    return (new_position, new_velocity)


def solution(mesh):
    cells = P("gx", "gy", "gz", None)
    lists = P("gx", "gy", "gz", None, None)
    vectors = P(None, "gx", "gy", "gz", None)
    return jax.shard_map(
        body,
        mesh=mesh,
        in_specs=(vectors, vectors, cells, cells, P(), lists, lists),
        out_specs=(vectors, vectors),
        check_vma=False,
    )
```
